32 devices in a mesh: tm: 8 (over z, x), col: 4 (over y, core).
Axes of the slice: x: 2, y: 2, z: 4, core: 2. Of those that a mesh axis runs over, the one named last changes fastest.
Arguments:
- observations: float32 [128, 64, 256], P('tm', 'col'), may hold values from -6 to 6
- band_index: int32 [128], P('tm'), may hold values from 0 to 3
- obs_mask: int32 [128], P('tm'), may hold values 0 or 1
- diffusivity: float32 [4, 256], replicated, may hold values from 0.005 to 0.05
- mode_correction_factors: float32 [4, 256, 256], replicated, may hold values from -0.01 to 0.06
- mode_backward_factors: float32 [4, 256, 256], replicated, may hold values from -0.01 to 1.01
- initial_mean: float32 [256], replicated, may hold values from -6 to 6
Outputs:
- filtered: float32 [128, 64, 256], P('tm', 'col')
- smoothed: float32 [128, 64, 256], P('tm', 'col')
The draws below stay inside these ranges and needn't reach their ends.
All inputs are finite; a program needn't handle non-finite values. No bound on the sum of `obs_mask` on one device may be relied on, other than what follows from the above.
Results may differ from the reference program's by a relative error of at most 0.0003.
Values sent between devices are 32-bit elements; how exact they have to be, the bound alone decides.
No kernel may reach another device: no remote copies, remote signals or barrier semaphores. Data moves between devices by JAX's collectives and lax.ppermute only.
A program may use at most 64 MiB of HBM per device.

```python
import math
import jax
import jax.numpy as jnp
from jax import lax

GRID = 16
STATE = 256
BANDS = 4
RECORDS = 64
STEPS = 128


def draw_mode_correction_factors(key, part):
    diag_key, off_key = jax.random.split(jax.random.fold_in(key, 11))
    diagonal = jnp.exp(jax.random.uniform(diag_key, (BANDS, STATE), jnp.float32, math.log(0.002), math.log(0.05)))
    noise = jnp.clip(jax.random.normal(off_key, (BANDS, STATE, STATE), jnp.float32), -3.0, 3.0)
    offdiag = 0.02 / math.sqrt(STATE) * noise
    return offdiag + diagonal[:, :, None] * jnp.eye(STATE, dtype=jnp.float32)


def draw_mode_backward_factors(key, part):
    pick_key, slow_key, fast_key, off_key = jax.random.split(jax.random.fold_in(key, 23), 4)
    slow_share = 0.5
    slow_cells = (jax.random.uniform(pick_key, (1, STATE), jnp.float32) < slow_share).astype(jnp.float32)
    slow_rate = jnp.exp(jax.random.uniform(slow_key, (BANDS, STATE), jnp.float32, math.log(0.1), math.log(2.0))) / STEPS
    fast_rate = 1.0 / jax.random.uniform(fast_key, (BANDS, STATE), jnp.float32, 30.0, 50.0)
    diagonal = jnp.exp(-(slow_cells * slow_rate + (1.0 - slow_cells) * fast_rate))
    noise = jnp.clip(jax.random.normal(off_key, (BANDS, STATE, STATE), jnp.float32), -3.0, 3.0)
    offdiag = 0.5 / (math.sqrt(STATE) * STEPS) * noise
    return offdiag + diagonal[:, :, None] * jnp.eye(STATE, dtype=jnp.float32)


def touch_ends(result, rng, least, top_value):
    extent = result.shape
    index_at = [jax.random.randint(jax.random.fold_in(rng, axis), (), 0, extent[axis]) for axis in range(len(extent))]
    result = result.at[tuple(index_at)].set(least)
    longest = extent.index(max(extent))
    index_at[longest] = (index_at[longest] + 1) % extent[longest]
    return result.at[tuple(index_at)].set(top_value)


def shard_levels(own_key, extent, cuts, least, high):
    loudness, own = 1.0, jax.random.fold_in(own_key, 6)
    for dim, parts in cuts:
        draws = jnp.exp(jax.random.uniform(jax.random.fold_in(own, dim), (parts,), jnp.float32, least / len(cuts), high / len(cuts)))
        loudness = loudness * jnp.repeat(draws, extent[dim] // parts).reshape([-1 if axis == dim else 1 for axis in range(len(extent))])
    return loudness


def bell_draw(key, shape, spread, reach, cuts=(), held_as=jnp.bfloat16):
    level = shard_levels(key, shape, cuts, -0.22, 0.18) if cuts else 1.0
    drawn = jax.random.normal(key, shape, jnp.float32) * spread * level
    return jnp.minimum(jnp.maximum(drawn, -reach), reach).astype(held_as)


def setup_inputs(seed: int = 0) -> dict:
    key_of = jax.random.split(jax.random.key(seed), 8)
    return {
        "observations": bell_draw(key_of[0], (STEPS, RECORDS, STATE), 1.0, 6.0, ((0, 8), (1, 4)), jnp.float32),
        "band_index": touch_ends(jax.random.randint(key_of[1], (STEPS,), 0, BANDS), jax.random.fold_in(key_of[1], 1), 0, BANDS - 1).astype(jnp.int32),
        "obs_mask": touch_ends((jax.random.randint(key_of[2], (STEPS,), 0, 32) < 1).astype(jnp.int32), jax.random.fold_in(key_of[2], 1), 0, 1),
        "diffusivity": jnp.clip(jnp.exp(jax.random.uniform(key_of[3], (BANDS, STATE), jnp.float32, math.log(0.005), math.log(0.05))), 0.005, 0.05),
        "mode_correction_factors": draw_mode_correction_factors(jax.random.fold_in(key_of[7], 71), 0),
        "mode_backward_factors": draw_mode_backward_factors(jax.random.fold_in(key_of[7], 71), 0),
        "initial_mean": bell_draw(key_of[6], (STATE,), 1.0, 6.0, (), jnp.float32),
    }


def accurate_matmul_result(first_factor, second_factor):
    return jnp.dot(first_factor, second_factor, precision=lax.Precision.HIGHEST)


def diffusion_matrices(diffusivity, side_cells):
    cell_count = side_cells * side_cells
    cell_ids = jnp.arange(cell_count)
    cell_row = cell_ids // side_cells
    cell_col = cell_ids % side_cells
    adjacent = (jnp.abs(cell_row[:, None] - cell_row[None, :]) + jnp.abs(cell_col[:, None] - cell_col[None, :])) == 1
    coupling = 0.5 * (diffusivity[:, :, None] + diffusivity[:, None, :]) * adjacent.astype(diffusivity.dtype)
    keeping = 1.0 - jnp.sum(coupling, axis=2)
    return coupling + keeping[:, :, None] * jnp.eye(cell_count, dtype=diffusivity.dtype)


def reference(observations, band_index, obs_mask, diffusivity, mode_correction_factors, mode_backward_factors, initial_mean):
    dynamics_operator_matrix = diffusion_matrices(diffusivity, GRID)
    start_rows = jnp.zeros((RECORDS, STATE), jnp.float32) + initial_mean[None, :]

    def filter_step(current_hidden_vector, argument_entries):
        entry_measurement, current_strip, current_measured_flag = argument_entries
        projected_field_vector = accurate_matmul_result(current_hidden_vector, dynamics_operator_matrix[current_strip])
        corrected_hidden_vector = projected_field_vector + current_measured_flag.astype(jnp.float32) * accurate_matmul_result(entry_measurement - projected_field_vector, mode_correction_factors[current_strip].T)
        return corrected_hidden_vector, (corrected_hidden_vector, projected_field_vector)

    _, (filtered, predicted) = lax.scan(filter_step, start_rows, (observations, band_index, obs_mask))
    next_predicted = jnp.concatenate([predicted[1:], jnp.zeros_like(predicted[:1])], axis=0)
    final_flag = (jnp.arange(STEPS) == STEPS - 1).astype(jnp.float32)

    def smooth_step(following_lines, argument_entries):
        current_average, projected_field_vector, current_strip, current_closing_flag = argument_entries
        current_refined_estimate = current_average + (1.0 - current_closing_flag) * accurate_matmul_result(following_lines - projected_field_vector, mode_backward_factors[current_strip].T)
        return current_refined_estimate, current_refined_estimate

    _, smoothed = lax.scan(smooth_step, jnp.zeros_like(start_rows), (filtered, next_predicted, band_index, final_flag), reverse=True)
    return filtered, smoothed
```

```python
import functools

import jax
import jax.numpy as jnp
from jax import lax
from jax.experimental import pallas as pl
from jax.experimental.pallas import tpu as pltpu
from jax.sharding import PartitionSpec as P

GRID = 16
SLOTS = 2
META = 8
MASK_AT, SLOT_AT, COUNT_AT = 32, 64, 96
BF, F32 = jnp.bfloat16, jnp.float32
VMEM_BYTES = 48 * 2**20


def halves(value):
    high = value.astype(BF)
    return high, (value - high.astype(F32)).astype(BF)


def dot(a, b):
    return jnp.dot(a, b, preferred_element_type=F32)


def rows_product(rows, high, low):
    m = rows.shape[0]
    rows_high, rows_low = halves(rows)
    both = dot(jnp.concatenate([rows_high, rows_low], 0), high)
    return both[:m] + both[m:] + dot(rows_high, low)


def from_cell(value, shift):
    cells = value.shape[-1]
    return pltpu.roll(value, (-shift) % cells, 1) if shift % cells else value


SHIFTS = (0, 1, -1, GRID, -GRID)


def stencils(diffusivity):
    cell = lax.broadcasted_iota(jnp.int32, diffusivity.shape, 1)
    cells = diffusivity.shape[1]
    row, column = cell // GRID, cell % GRID
    inside = {1: column < GRID - 1, -1: column > 0, GRID: row < cells // GRID - 1, -GRID: row > 0}
    parts = {
        s: jnp.where(inside[s], 0.5 * (diffusivity + from_cell(diffusivity, s)), 0.0)
        for s in SHIFTS[1:]
    }
    parts[0] = 1.0 - (parts[1] + parts[-1] + parts[GRID] + parts[-GRID])
    return parts


def two_step_shifts():
    return sorted({a + b for a in SHIFTS for b in SHIFTS}, key=abs)


def tree_sum(terms):
    while len(terms) > 1:
        terms = [sum(terms[i + 1 : i + 2], terms[i]) for i in range(0, len(terms), 2)]
    return terms[0]


def apply_stencil(weights, shifts, value):
    return tree_sum([weights[k : k + 1] * from_cell(value, s) for k, s in enumerate(shifts)])


def tables_kernel(bands, diffusivity, gain, back, one, two, gain_high, gain_low, back_high, back_low, pair_high, pair_low):
    first = stencils(diffusivity[...])
    for b in range(bands):
        for k, s in enumerate(SHIFTS):
            one[b, k : k + 1, :] = first[s][b : b + 1]
    for b in range(bands):
        for c in range(bands):
            total = {}
            for s in SHIFTS:
                for r in SHIFTS:
                    term = first[s][c : c + 1] * from_cell(first[r][b : b + 1], s)
                    total[s + r] = total[s + r] + term if s + r in total else term
            for k, s in enumerate(two_step_shifts()):
                two[b * bands + c, k : k + 1, :] = total[s]
    for b in range(bands):
        gain_high[b], gain_low[b] = halves(gain[b].T)
        back_high[b], back_low[b] = halves(back[b].T)

    def pair(i, carry):
        b, c = i // bands, i % bands
        high, low = back_high[b], back_low[b]
        product = dot(high, back_high[c]) + (dot(low, back_high[c]) + dot(high, back_low[c]))
        pair_high[i], pair_low[i] = halves(product)
        return carry

    lax.fori_loop(0, bands * bands, pair, 0, unroll=4)


def pack_kernel(bands, band, mask, observations, diffusivity, gain, back, message, one, gain_here, back_here, delta, sem):
    steps, records, states = observations.shape
    lane = lax.broadcasted_iota(jnp.int32, (META, states), 1)
    meta = jnp.zeros((META, states), F32)
    count = jnp.int32(0)
    for t in range(steps):
        seen = mask[t]
        put = lambda at, value: jnp.where(lane == at + t, value.astype(F32), meta)
        meta = put(0, band[t])
        meta = put(MASK_AT, seen)
        meta = put(SLOT_AT, count)

        @pl.when((seen > 0) & (count < SLOTS))
        def _(t=t, at=count):
            message[pl.ds(at * records, records), :] = observations[t]

        count = count + seen
    message[SLOTS * records :, :] = jnp.where(lane == COUNT_AT, count.astype(F32), meta)

    for slot in range(SLOTS):

        @pl.when(count <= slot)
        def _(slot=slot):
            message[slot * records : (slot + 1) * records, :] = jnp.zeros((records, states), F32)

    @pl.when(count > SLOTS)
    def _():
        copies = [pltpu.make_async_copy(a, b, sem.at[i]) for i, (a, b) in enumerate(((gain, gain_here), (back, back_here)))]
        for copy in copies:
            copy.start()
        first = stencils(diffusivity[...])
        for b in range(bands):
            for k, s in enumerate(SHIFTS):
                one[b, k : k + 1, :] = first[s][b : b + 1]
        for copy in copies:
            copy.wait()

        def times(rows, matrix):
            return lax.dot_general(
                rows, matrix, (((1,), (1,)), ((), ())), precision=lax.Precision.HIGHEST, preferred_element_type=F32
            )

        def forward(t, x):
            p = apply_stencil(one[band[t]], SHIFTS, x)
            delta[t] = mask[t].astype(F32) * times(observations[t] - p, gain_here[band[t]])
            return p + delta[t]

        zeros = jnp.zeros((records, states), F32)
        message[0:records, :] = lax.fori_loop(0, steps, forward, zeros)

        def backward(i, r):
            t = steps - 1 - i
            return times(r, back_here[band[t]]) + delta[t]

        message[records : 2 * records, :] = lax.fori_loop(0, steps, backward, zeros)


def main_kernel(
    bands,
    devices,
    fields,
    pieces,
    me_ref,
    band_own,
    mask_own,
    observations,
    start,
    *refs,
):
    parts, refs = refs[:pieces], refs[pieces:]
    (one, two, gain_high, gain_low, back_high, back_low, pair_high, pair_low), refs = refs[:8], refs[8:]
    filtered, smoothed, inbox, meta, table, delta, sem = refs
    steps, records, states = observations.shape
    rows = parts[0].shape[0] // (devices // pieces)
    me = me_ref[0]
    for i, part in enumerate(parts):
        each = part.shape[0]
        inbox[i * each : (i + 1) * each, :] = part[...]
    for k in range(devices):
        at = k * rows + SLOTS * records
        meta[k : k + 1, :] = inbox[at : at + 1, :].astype(jnp.int32)
    copy = pltpu.make_async_copy(meta, table, sem)
    copy.start()
    copy.wait()

    def place(block):
        apart = lax.bitwise_xor(block, me)
        found, scale = jnp.int32(0), 1
        for shift, width in reversed(fields):
            found = found + lax.bitwise_and(lax.shift_right_logical(apart, shift), width - 1) * scale
            scale *= width
        return found

    def step(b, x):
        return apply_stencil(one[b], SHIFTS, x)

    def innovation(b, difference):
        return rows_product(difference, gain_high[b], gain_low[b])

    def back(b, r):
        return rows_product(r, back_high[b], back_low[b])

    def filter_own(x):
        def body(t, x):
            b = band_own[t]
            p = step(b, x)

            def seen(p):
                change = innovation(b, observations[t] - p)
                delta[me * steps + t] = change
                return p + change

            x = lax.cond(mask_own[t] > 0, seen, lambda p: p, p)
            filtered[t] = x
            return x

        return lax.fori_loop(0, steps, body, x)

    def filter_block(block, x):
        at = place(block)
        packed = table[at, COUNT_AT] > SLOTS

        def pair(j, x):
            t = 2 * j
            b, c = table[at, t], table[at, t + 1]
            m, n = table[at, MASK_AT + t], table[at, MASK_AT + t + 1]

            def single(b, m, t, x):
                p = step(b, x)

                def seen(p):
                    row = pl.multiple_of(at * rows + lax.rem(table[at, SLOT_AT + t], SLOTS) * records, 8)
                    y = jnp.where(packed, 0.0, inbox[pl.ds(row, records), :])
                    change = innovation(b, y - p)
                    delta[block * steps + t] = change
                    return p + change

                return lax.cond(m > 0, seen, lambda p: p, p)

            return lax.cond(
                m + n > 0,
                lambda x: single(c, n, t + 1, single(b, m, t, x)),
                lambda x: apply_stencil(two[b * bands + c], two_step_shifts(), x),
                x,
            )

        x = lax.fori_loop(0, steps // 2, pair, x)
        row = pl.multiple_of(at * rows, 8)
        return lax.cond(packed, lambda x: x + inbox[pl.ds(row, records), :], lambda x: x, x)

    x = jnp.broadcast_to(start[...], (records, states))
    lax.fori_loop(
        0,
        devices,
        lambda block, x: lax.cond(block == me, filter_own, functools.partial(filter_block, block), x),
        x,
    )

    def smooth_block(i, r):
        block = devices - 1 - i
        at = place(block)

        def pair(j, r):
            t = steps - 2 - 2 * j
            b, c = table[at, t], table[at, t + 1]
            m, n = table[at, MASK_AT + t], table[at, MASK_AT + t + 1]

            def added(m, t, r):
                return lax.cond(m > 0, lambda r: r + delta[block * steps + t], lambda r: r, r)

            r = lax.cond(
                n > 0,
                lambda r: back(b, added(n, t + 1, back(c, r))),
                lambda r: rows_product(r, pair_high[c * bands + b], pair_low[c * bands + b]),
                r,
            )
            return added(m, t, r)

        r = lax.fori_loop(0, steps // 2, pair, r)
        row = pl.multiple_of(at * rows + records, 8)
        return lax.cond(table[at, COUNT_AT] > SLOTS, lambda r: r + inbox[pl.ds(row, records), :], lambda r: r, r)

    r = lax.fori_loop(0, devices - 1 - me, smooth_block, jnp.zeros((records, states), F32))

    def smooth_own(i, r):
        t = steps - 1 - i
        e = back(band_own[t], r)
        smoothed[t] = filtered[t] + e
        return lax.cond(mask_own[t] > 0, lambda e: e + delta[me * steps + t], lambda e: e, e)

    lax.fori_loop(0, steps, smooth_own, r)


def whole(memory=pltpu.VMEM):
    return pl.BlockSpec(memory_space=memory)


def exchange(message, devices):
    bits = devices.bit_length() - 1
    widths = ([1] if bits % 2 else []) + [2] * (bits // 2)
    pieces, fields, low = [message], [], bits
    for width in widths:
        low -= width
        held = jnp.concatenate(pieces, 0)
        pieces = [held] + [
            lax.ppermute(held, "tm", [(i, i ^ (k << low)) for i in range(devices)]) for k in range(1, 1 << width)
        ]
        fields = [(low, 1 << width)] + fields
    return pieces, fields


def shards(observations, band_index, obs_mask, diffusivity, gain, back, initial_mean):
    steps, records, states = observations.shape
    bands = diffusivity.shape[0]
    devices = lax.axis_size("tm")
    rows = SLOTS * records + META
    params = pltpu.CompilerParams(vmem_limit_bytes=VMEM_BYTES)
    shape = jax.ShapeDtypeStruct
    message = pl.pallas_call(
        functools.partial(pack_kernel, bands),
        out_shape=shape((rows, states), F32),
        in_specs=[whole(pltpu.SMEM)] * 2 + [whole()] * 2 + [whole(pl.ANY)] * 2,
        out_specs=whole(),
        scratch_shapes=[
            pltpu.VMEM((bands, 8, states), F32),
            pltpu.VMEM((bands, states, states), F32),
            pltpu.VMEM((bands, states, states), F32),
            pltpu.VMEM((steps, records, states), F32),
            pltpu.SemaphoreType.DMA((2,)),
        ],
        compiler_params=params,
        name="pack_message",
    )(band_index, obs_mask, observations, diffusivity, gain, back)
    pieces, fields = exchange(message, devices)
    matrix = lambda count: shape((count, states, states), BF)
    tables = pl.pallas_call(
        functools.partial(tables_kernel, bands),
        out_shape=[shape((bands, 8, states), F32), shape((bands * bands, 16, states), F32)]
        + [matrix(bands)] * 4
        + [matrix(bands * bands)] * 2,
        in_specs=[whole()] * 3,
        out_specs=[whole()] * 8,
        compiler_params=params,
        cost_estimate=pl.CostEstimate(flops=6 * bands**2 * states**3, bytes_accessed=8 * 2**20, transcendentals=0),
        name="tables",
    )(diffusivity, gain, back)
    me = lax.axis_index("tm").astype(jnp.int32)[None]
    out = shape((steps, records, states), F32)
    return pl.pallas_call(
        functools.partial(main_kernel, bands, devices, fields, len(pieces)),
        out_shape=[out, out],
        in_specs=[whole(pltpu.SMEM)] * 3 + [whole()] * (2 + len(pieces) + len(tables)),
        out_specs=[whole()] * 2,
        scratch_shapes=[
            pltpu.VMEM((devices * rows, states), F32),
            pltpu.VMEM((devices, states), jnp.int32),
            pltpu.SMEM((devices, states), jnp.int32),
            pltpu.VMEM((devices * steps, records, states), F32),
            pltpu.SemaphoreType.DMA,
        ],
        compiler_params=params,
        name="filter_and_smooth",
    )(me, band_index, obs_mask, observations, initial_mean[None, :], *pieces, *tables)


def solution(mesh):
    return jax.shard_map(
        shards,
        mesh=mesh,
        in_specs=(P("tm", "col", None), P("tm"), P("tm"), P(), P(), P(), P()),
        out_specs=(P("tm", "col", None), P("tm", "col", None)),
        check_vma=False,
    )
```

```python
import functools

import jax
import jax.numpy as jnp
from jax import lax
from jax.experimental import pallas as pl
from jax.experimental.pallas import tpu as pltpu
from jax.sharding import PartitionSpec as P

GRID = 16
SLOTS = 3
META = 8
MASK_AT, SLOT_AT, COUNT_AT = 32, 64, 96
BF, F32 = jnp.bfloat16, jnp.float32
VMEM_BYTES = 24 * 2**20
PACK_VMEM_BYTES = 60 * 2**20


def halves(value):
    high = value.astype(BF)
    return high, (value - high.astype(F32)).astype(BF)


def dot(a, b):
    return jnp.dot(a, b, preferred_element_type=F32)


def rows_product(rows, high, low):
    m = rows.shape[0]
    rows_high, rows_low = halves(rows)
    both = dot(jnp.concatenate([rows_high, rows_low], 0), high)
    return both[:m] + both[m:] + dot(rows_high, low)


def from_cell(value, shift):
    cells = value.shape[-1]
    return pltpu.roll(value, (-shift) % cells, 1) if shift % cells else value


SHIFTS = (0, 1, -1, GRID, -GRID)


def stencils(diffusivity):
    cell = lax.broadcasted_iota(jnp.int32, diffusivity.shape, 1)
    cells = diffusivity.shape[1]
    row, column = cell // GRID, cell % GRID
    inside = {1: column < GRID - 1, -1: column > 0, GRID: row < cells // GRID - 1, -GRID: row > 0}
    parts = {
        s: jnp.where(inside[s], 0.5 * (diffusivity + from_cell(diffusivity, s)), 0.0)
        for s in SHIFTS[1:]
    }
    parts[0] = 1.0 - (parts[1] + parts[-1] + parts[GRID] + parts[-GRID])
    return parts


def two_step_shifts():
    return sorted({a + b for a in SHIFTS for b in SHIFTS}, key=abs)


def tree_sum(terms):
    while len(terms) > 1:
        terms = [sum(terms[i + 1 : i + 2], terms[i]) for i in range(0, len(terms), 2)]
    return terms[0]


def apply_stencil(weights, shifts, value):
    return tree_sum([weights[k : k + 1] * from_cell(value, s) for k, s in enumerate(shifts)])


def tables_kernel(bands, diffusivity, gain, back, one, two, gain_high, gain_low, back_high, back_low):
    first = stencils(diffusivity[...])
    for b in range(bands):
        for k, s in enumerate(SHIFTS):
            one[b, k : k + 1, :] = first[s][b : b + 1]
    for b in range(bands):
        for c in range(bands):
            total = {}
            for s in SHIFTS:
                for r in SHIFTS:
                    term = first[s][c : c + 1] * from_cell(first[r][b : b + 1], s)
                    total[s + r] = total[s + r] + term if s + r in total else term
            for k, s in enumerate(two_step_shifts()):
                two[b * bands + c, k : k + 1, :] = total[s]
    for b in range(bands):
        gain_high[b], gain_low[b] = halves(gain[b].T)
        back_high[b], back_low[b] = halves(back[b].T)


def pairs_kernel(bands, back_high, back_low, pair_high, pair_low):
    def pair(i, carry):
        b, c = i // bands, i % bands
        high, low = back_high[b], back_low[b]
        product = dot(high, back_high[c]) + (dot(low, back_high[c]) + dot(high, back_low[c]))
        pair_high[i], pair_low[i] = halves(product)
        return carry

    lax.fori_loop(0, bands * bands, pair, 0, unroll=4)


def pack_kernel(
    bands, band_far, mask_far, observations_far, diffusivity_far, gain, back, message, band, mask, observations, diffusivity, one,
    gain_here, back_here, delta, sem,
):
    steps, records, states = observations.shape
    near = (band, mask, observations, diffusivity)
    copies = [
        pltpu.make_async_copy(a, b, sem.at[i])
        for i, (a, b) in enumerate(zip((band_far, mask_far, observations_far, diffusivity_far), near))
    ]
    for copy in copies:
        copy.start()
    for copy in copies:
        copy.wait()
    lane = lax.broadcasted_iota(jnp.int32, (META, states), 1)
    meta = jnp.zeros((META, states), F32)
    count = jnp.int32(0)
    for t in range(steps):
        seen = mask[t]
        put = lambda at, value: jnp.where(lane == at + t, value.astype(F32), meta)
        meta = put(0, band[t])
        meta = put(MASK_AT, seen)
        meta = put(SLOT_AT, count)

        @pl.when((seen > 0) & (count < SLOTS))
        def _(t=t, at=count):
            message[pl.ds(at * records, records), :] = observations[t]

        count = count + seen
    message[SLOTS * records :, :] = jnp.where(lane == COUNT_AT, count.astype(F32), meta)

    for slot in range(SLOTS):

        @pl.when(count <= slot)
        def _(slot=slot):
            message[slot * records : (slot + 1) * records, :] = jnp.zeros((records, states), F32)

    @pl.when(count > SLOTS)
    def _():
        copies = [pltpu.make_async_copy(a, b, sem.at[i]) for i, (a, b) in enumerate(((gain, gain_here), (back, back_here)))]
        for copy in copies:
            copy.start()
        first = stencils(diffusivity[...])
        for b in range(bands):
            for k, s in enumerate(SHIFTS):
                one[b, k : k + 1, :] = first[s][b : b + 1]
        for copy in copies:
            copy.wait()

        def times(rows, matrix):
            return lax.dot_general(
                rows, matrix, (((1,), (1,)), ((), ())), precision=lax.Precision.HIGHEST, preferred_element_type=F32
            )

        def forward(t, x):
            p = apply_stencil(one[band[t]], SHIFTS, x)
            delta[t] = mask[t].astype(F32) * times(observations[t] - p, gain_here[band[t]])
            return p + delta[t]

        zeros = jnp.zeros((records, states), F32)
        message[0:records, :] = lax.fori_loop(0, steps, forward, zeros)

        def backward(i, r):
            t = steps - 1 - i
            return times(r, back_here[band[t]]) + delta[t]

        message[records : 2 * records, :] = lax.fori_loop(0, steps, backward, zeros)


def main_kernel(
    bands,
    devices,
    fields,
    pieces,
    me_ref,
    band_own,
    mask_own,
    observations,
    start,
    *refs,
):
    parts, refs = refs[:pieces], refs[pieces:]
    (one, two, gain_high, gain_low, back_high, back_low, pair_high, pair_low), refs = refs[:8], refs[8:]
    filtered, smoothed, inbox, meta, table, delta, sem = refs
    steps, records, states = observations.shape
    rows = parts[0].shape[0] // (devices // pieces)
    me = me_ref[0]
    for i, part in enumerate(parts):
        each = part.shape[0]
        inbox[i * each : (i + 1) * each, :] = part[...]
    for k in range(devices):
        at = k * rows + SLOTS * records
        meta[k : k + 1, :] = inbox[at : at + 1, :].astype(jnp.int32)
    copy = pltpu.make_async_copy(meta, table, sem)
    copy.start()
    copy.wait()

    def place(block):
        apart = lax.bitwise_xor(block, me)
        found, scale = jnp.int32(0), 1
        for shift, width in reversed(fields):
            found = found + lax.bitwise_and(lax.shift_right_logical(apart, shift), width - 1) * scale
            scale *= width
        return found

    def step(b, x):
        return apply_stencil(one[b], SHIFTS, x)

    def innovation(b, difference):
        return rows_product(difference, gain_high[b], gain_low[b])

    def back(b, r):
        return rows_product(r, back_high[b], back_low[b])

    def filter_own(x):
        def body(t, x):
            b = band_own[t]
            p = step(b, x)

            def seen(p):
                change = innovation(b, observations[t] - p)
                delta[me * steps + t] = change
                return p + change

            x = lax.cond(mask_own[t] > 0, seen, lambda p: p, p)
            filtered[t] = x
            return x

        return lax.fori_loop(0, steps, body, x)

    def filter_block(block, x):
        at = place(block)
        packed = table[at, COUNT_AT] > SLOTS

        def pair(j, x):
            t = 2 * j
            b, c = table[at, t], table[at, t + 1]
            m, n = table[at, MASK_AT + t], table[at, MASK_AT + t + 1]

            def single(b, m, t, x):
                p = step(b, x)

                def seen(p):
                    row = pl.multiple_of(at * rows + lax.rem(table[at, SLOT_AT + t], SLOTS) * records, 8)
                    y = jnp.where(packed, 0.0, inbox[pl.ds(row, records), :])
                    change = innovation(b, y - p)
                    delta[block * steps + t] = change
                    return p + change

                return lax.cond(m > 0, seen, lambda p: p, p)

            return lax.cond(
                m + n > 0,
                lambda x: single(c, n, t + 1, single(b, m, t, x)),
                lambda x: apply_stencil(two[b * bands + c], two_step_shifts(), x),
                x,
            )

        x = lax.fori_loop(0, steps // 2, pair, x)
        row = pl.multiple_of(at * rows, 8)
        return lax.cond(packed, lambda x: x + inbox[pl.ds(row, records), :], lambda x: x, x)

    x = jnp.broadcast_to(start[...], (records, states))
    lax.fori_loop(
        0,
        devices,
        lambda block, x: lax.cond(block == me, filter_own, functools.partial(filter_block, block), x),
        x,
    )

    def smooth_block(i, r):
        block = devices - 1 - i
        at = place(block)

        def pair(j, r):
            t = steps - 2 - 2 * j
            b, c = table[at, t], table[at, t + 1]
            m, n = table[at, MASK_AT + t], table[at, MASK_AT + t + 1]

            def added(m, t, r):
                return lax.cond(m > 0, lambda r: r + delta[block * steps + t], lambda r: r, r)

            r = lax.cond(
                n > 0,
                lambda r: back(b, added(n, t + 1, back(c, r))),
                lambda r: rows_product(r, pair_high[c * bands + b], pair_low[c * bands + b]),
                r,
            )
            return added(m, t, r)

        r = lax.fori_loop(0, steps // 2, pair, r)
        row = pl.multiple_of(at * rows + records, 8)
        return lax.cond(table[at, COUNT_AT] > SLOTS, lambda r: r + inbox[pl.ds(row, records), :], lambda r: r, r)

    r = lax.fori_loop(0, devices - 1 - me, smooth_block, jnp.zeros((records, states), F32))

    def smooth_own(i, r):
        t = steps - 1 - i
        e = back(band_own[t], r)
        smoothed[t] = filtered[t] + e
        return lax.cond(mask_own[t] > 0, lambda e: e + delta[me * steps + t], lambda e: e, e)

    lax.fori_loop(0, steps, smooth_own, r)


def whole(memory=pltpu.VMEM):
    return pl.BlockSpec(memory_space=memory)


def xor_round(held, low, width, devices):
    return [held] + [
        lax.ppermute(held, "tm", [(i, i ^ (k << low)) for i in range(devices)]) for k in range(1, 1 << width)
    ]


def shards(observations, band_index, obs_mask, diffusivity, gain, back, initial_mean):
    steps, records, states = observations.shape
    bands = diffusivity.shape[0]
    devices = lax.axis_size("tm")
    rows = SLOTS * records + META
    params = pltpu.CompilerParams(vmem_limit_bytes=VMEM_BYTES)
    shape = jax.ShapeDtypeStruct
    message = pl.pallas_call(
        functools.partial(pack_kernel, bands),
        out_shape=shape((rows, states), F32),
        in_specs=[whole(pltpu.HBM)] * 6,
        out_specs=whole(),
        scratch_shapes=[
            pltpu.SMEM((steps,), jnp.int32),
            pltpu.SMEM((steps,), jnp.int32),
            pltpu.VMEM((steps, records, states), F32),
            pltpu.VMEM((bands, states), F32),
            pltpu.VMEM((bands, 8, states), F32),
            pltpu.VMEM((bands, states, states), F32),
            pltpu.VMEM((bands, states, states), F32),
            pltpu.VMEM((steps, records, states), F32),
            pltpu.SemaphoreType.DMA((4,)),
        ],
        compiler_params=pltpu.CompilerParams(vmem_limit_bytes=PACK_VMEM_BYTES),
        name="pack_message",
    )(band_index, obs_mask, observations, diffusivity, gain, back)
    matrix = lambda count: shape((count, states, states), BF)
    cost = lambda flops: pl.CostEstimate(flops=flops, bytes_accessed=4 * 2**20, transcendentals=0)

    def make_tables():
        return pl.pallas_call(
            functools.partial(tables_kernel, bands),
            out_shape=[shape((bands, 8, states), F32), shape((bands * bands, 16, states), F32)] + [matrix(bands)] * 4,
            in_specs=[whole()] * 3,
            out_specs=[whole()] * 6,
            compiler_params=params,
            cost_estimate=cost(2**28),
            name="tables",
        )(diffusivity, gain, back)

    def make_pairs(back_high, back_low):
        return pl.pallas_call(
            functools.partial(pairs_kernel, bands),
            out_shape=[matrix(bands * bands)] * 2,
            in_specs=[whole()] * 2,
            out_specs=[whole()] * 2,
            compiler_params=params,
            cost_estimate=cost(6 * bands**2 * states**3),
            name="pairs",
        )(back_high, back_low)

    bits = devices.bit_length() - 1
    pieces, fields, low, tables = [message], [], bits, None
    for width in [1] * (bits % 2) + [2] * (bits // 2):
        low -= width
        held = jnp.concatenate(pieces, 0)
        if fields and tables is None:
            tables = make_tables()
            held, tables = lax.optimization_barrier((held, tables))
        pieces = xor_round(held, low, width, devices)
        fields = [(low, 1 << width)] + fields
    tables = make_tables() if tables is None else tables
    tables = [*tables, *make_pairs(*tables[4:6])]
    me = lax.axis_index("tm").astype(jnp.int32)[None]
    out = shape((steps, records, states), F32)
    return pl.pallas_call(
        functools.partial(main_kernel, bands, devices, fields, len(pieces)),
        out_shape=[out, out],
        in_specs=[whole(pltpu.SMEM)] * 3 + [whole()] * (2 + len(pieces) + len(tables)),
        out_specs=[whole()] * 2,
        scratch_shapes=[
            pltpu.VMEM((devices * rows, states), F32),
            pltpu.VMEM((devices, states), jnp.int32),
            pltpu.SMEM((devices, states), jnp.int32),
            pltpu.VMEM((devices * steps, records, states), F32),
            pltpu.SemaphoreType.DMA,
        ],
        compiler_params=params,
        name="filter_and_smooth",
    )(me, band_index, obs_mask, observations, initial_mean[None, :], *pieces, *tables)


def solution(mesh):
    return jax.shard_map(
        shards,
        mesh=mesh,
        in_specs=(P("tm", "col", None), P("tm"), P("tm"), P(), P(), P(), P()),
        out_specs=(P("tm", "col", None), P("tm", "col", None)),
        check_vma=False,
    )
```

```python
import functools

import jax
import jax.numpy as jnp
from jax import lax
from jax.experimental import pallas as pl
from jax.experimental.pallas import tpu as pltpu
from jax.sharding import PartitionSpec as P

GRID = 16
SLOTS = 3
META = 8
MASK_AT, SLOT_AT, COUNT_AT = 32, 64, 96
BF, F32 = jnp.bfloat16, jnp.float32
VMEM_BYTES = 40 * 2**20
QUADS_BYTES = 2**24
PACK_VMEM_BYTES = 60 * 2**20


def halves(value):
    high = value.astype(BF)
    return high, (value - high.astype(F32)).astype(BF)


def dot(a, b):
    return jnp.dot(a, b, preferred_element_type=F32)


def rows_product(rows, high, low):
    m = rows.shape[0]
    rows_high, rows_low = halves(rows)
    both = dot(jnp.concatenate([rows_high, rows_low], 0), high)
    return both[:m] + both[m:] + dot(rows_high, low)


def from_cell(value, shift):
    cells = value.shape[-1]
    return pltpu.roll(value, (-shift) % cells, 1) if shift % cells else value


SHIFTS = (0, 1, -1, GRID, -GRID)


def stencils(diffusivity):
    cell = lax.broadcasted_iota(jnp.int32, diffusivity.shape, 1)
    cells = diffusivity.shape[1]
    row, column = cell // GRID, cell % GRID
    inside = {1: column < GRID - 1, -1: column > 0, GRID: row < cells // GRID - 1, -GRID: row > 0}
    parts = {
        s: jnp.where(inside[s], 0.5 * (diffusivity + from_cell(diffusivity, s)), 0.0)
        for s in SHIFTS[1:]
    }
    parts[0] = 1.0 - (parts[1] + parts[-1] + parts[GRID] + parts[-GRID])
    return parts


def two_step_shifts():
    return sorted({a + b for a in SHIFTS for b in SHIFTS}, key=abs)


def tree_sum(terms):
    while len(terms) > 1:
        terms = [sum(terms[i + 1 : i + 2], terms[i]) for i in range(0, len(terms), 2)]
    return terms[0]


def apply_stencil(weights, shifts, value):
    return tree_sum([weights[k : k + 1] * from_cell(value, s) for k, s in enumerate(shifts)])


def tables_kernel(bands, diffusivity, gain, back, one, two, gain_high, gain_low, back_high, back_low):
    first = stencils(diffusivity[...])
    for b in range(bands):
        for k, s in enumerate(SHIFTS):
            one[b, k : k + 1, :] = first[s][b : b + 1]
    for b in range(bands):
        for c in range(bands):
            total = {}
            for s in SHIFTS:
                for r in SHIFTS:
                    term = first[s][c : c + 1] * from_cell(first[r][b : b + 1], s)
                    total[s + r] = total[s + r] + term if s + r in total else term
            for k, s in enumerate(two_step_shifts()):
                two[b * bands + c, k : k + 1, :] = total[s]
    for b in range(bands):
        gain_high[b], gain_low[b] = halves(gain[b].T)
        back_high[b], back_low[b] = halves(back[b].T)


def pairs_kernel(bands, back_high, back_low, pair_high, pair_low):
    def pair(i, carry):
        b, c = i // bands, i % bands
        high, low = back_high[b], back_low[b]
        product = dot(high, back_high[c]) + (dot(low, back_high[c]) + dot(high, back_low[c]))
        pair_high[i], pair_low[i] = halves(product)
        return carry

    lax.fori_loop(0, bands * bands, pair, 0, unroll=4)


def pack_kernel(
    bands, band_far, mask_far, observations_far, diffusivity_far, gain, back, message, band, mask, observations, diffusivity, one,
    gain_here, back_here, delta, sem,
):
    steps, records, states = observations.shape
    near = (band, mask, observations, diffusivity)
    copies = [
        pltpu.make_async_copy(a, b, sem.at[i])
        for i, (a, b) in enumerate(zip((band_far, mask_far, observations_far, diffusivity_far), near))
    ]
    for copy in copies:
        copy.start()
    for copy in copies:
        copy.wait()
    lane = lax.broadcasted_iota(jnp.int32, (META, states), 1)
    meta = jnp.zeros((META, states), F32)
    count = jnp.int32(0)
    for t in range(steps):
        seen = mask[t]
        put = lambda at, value: jnp.where(lane == at + t, value.astype(F32), meta)
        meta = put(0, band[t])
        meta = put(MASK_AT, seen)
        meta = put(SLOT_AT, count)

        @pl.when((seen > 0) & (count < SLOTS))
        def _(t=t, at=count):
            message[pl.ds(at * records, records), :] = observations[t]

        count = count + seen
    message[SLOTS * records :, :] = jnp.where(lane == COUNT_AT, count.astype(F32), meta)

    for slot in range(SLOTS):

        @pl.when(count <= slot)
        def _(slot=slot):
            message[slot * records : (slot + 1) * records, :] = jnp.zeros((records, states), F32)

    @pl.when(count > SLOTS)
    def _():
        copies = [pltpu.make_async_copy(a, b, sem.at[i]) for i, (a, b) in enumerate(((gain, gain_here), (back, back_here)))]
        for copy in copies:
            copy.start()
        first = stencils(diffusivity[...])
        for b in range(bands):
            for k, s in enumerate(SHIFTS):
                one[b, k : k + 1, :] = first[s][b : b + 1]
        for copy in copies:
            copy.wait()

        def times(rows, matrix):
            return lax.dot_general(
                rows, matrix, (((1,), (1,)), ((), ())), precision=lax.Precision.HIGHEST, preferred_element_type=F32
            )

        def forward(t, x):
            p = apply_stencil(one[band[t]], SHIFTS, x)
            delta[t] = mask[t].astype(F32) * times(observations[t] - p, gain_here[band[t]])
            return p + delta[t]

        zeros = jnp.zeros((records, states), F32)
        message[0:records, :] = lax.fori_loop(0, steps, forward, zeros)

        def backward(i, r):
            t = steps - 1 - i
            return times(r, back_here[band[t]]) + delta[t]

        message[records : 2 * records, :] = lax.fori_loop(0, steps, backward, zeros)


def main_kernel(
    bands,
    devices,
    fields,
    pieces,
    observations,
    start,
    *refs,
):
    parts, refs = refs[:pieces], refs[pieces:]
    (one, two, gain_high, gain_low, back_high, back_low, pair_high, pair_low), refs = refs[:8], refs[8:]
    (filtered_far, smoothed_far, filtered, smoothed, out_sem), refs = refs[:5], refs[5:]
    (inbox, meta, table, delta, sem), quads = refs[:5], refs[5:]
    steps, records, states = observations.shape
    rows = parts[0].shape[0] // (devices // pieces)
    me = lax.axis_index("tm")

    def place(apart):
        found, scale = jnp.int32(0), 1
        for shift, width in reversed(fields):
            found = found + lax.bitwise_and(lax.shift_right_logical(apart, shift), width - 1) * scale
            scale *= width
        return found

    def apart_at(position):
        apart, position = 0, int(position)
        for shift, width in reversed(fields):
            apart |= (position % width) << shift
            position //= width
        return apart

    each = parts[0].shape[0]
    for k in range(devices):
        at = k * rows + SLOTS * records - k * rows // each * each
        block = lax.bitwise_xor(me, apart_at(k))
        meta[pl.ds(block, 1), :] = parts[k * rows // each][at : at + 1, :].astype(jnp.int32)
    copy = pltpu.make_async_copy(meta, table, sem)
    copy.start()
    for i, part in enumerate(parts):
        inbox[i * each : (i + 1) * each, :] = part[...]
    copy.wait()

    def step(b, x):
        return apply_stencil(one[b], SHIFTS, x)

    def two_steps(b, c, x):
        return apply_stencil(two[b * bands + c], two_step_shifts(), x)

    def innovation(b, difference):
        return rows_product(difference, gain_high[b], gain_low[b])

    def back(b, r):
        return rows_product(r, back_high[b], back_low[b])

    def back_two(c, b, r):
        return rows_product(r, pair_high[c * bands + b], pair_low[c * bands + b])

    def regimes(quad):
        block, t = quad // (steps // 4), lax.rem(quad, steps // 4) * 4
        return block, t, [table[block, t + k] for k in range(4)], [table[block, MASK_AT + t + k] for k in range(4)]

    def prepare(quad, b):
        if quads:
            left, right = b[3] * bands + b[2], b[1] * bands + b[0]
            high, low = pair_high[left], pair_low[left]
            product = dot(high, pair_high[right]) + (dot(low, pair_high[right]) + dot(high, pair_low[right]))
            quads[0][quad], quads[1][quad] = halves(product)

    def packed(block):
        return table[block, COUNT_AT] > SLOTS

    def filter_quad(quad, x):
        block, t, b, m = regimes(quad)
        own = block == me
        ends = packed(block) & (t == steps - 4)
        seen = (m[0] + m[1] + m[2] + m[3] > 0) | ends

        def plain(x):
            prepare(quad, b)
            return two_steps(b[2], b[3], two_steps(b[0], b[1], x))

        def plain_own(x):
            prepare(quad, b)
            filtered[t] = step(b[0], x)
            x = two_steps(b[0], b[1], x)
            filtered[t + 1] = x
            filtered[t + 2] = step(b[2], x)
            x = two_steps(b[2], b[3], x)
            filtered[t + 3] = x
            return x

        def observed(k, y, p):
            change = innovation(b[k], y - p)
            delta[quad * 4 + k] = change
            return p + change

        def seen_own(x):
            for k in range(4):
                p = step(b[k], x)
                x = lax.cond(m[k] > 0, lambda p, k=k: observed(k, observations[t + k], p), lambda p: p, p)
                filtered[t + k] = x
            return x

        def seen_other(x):
            first = pl.multiple_of(place(lax.bitwise_xor(block, me)) * rows, 8)

            def sent(k, p):
                slot = lax.rem(table[block, SLOT_AT + t + k], SLOTS)
                y = inbox[pl.ds(pl.multiple_of(first + slot * records, 8), records), :]
                return observed(k, jnp.where(packed(block), 0.0, y), p)

            def singles(k, x):
                for k in (k, k + 1):
                    x = lax.cond(m[k] > 0, lambda p, k=k: sent(k, p), lambda p: p, step(b[k], x))
                return x

            for k in (0, 2):
                x = lax.cond(
                    m[k] + m[k + 1] > 0, lambda x, k=k: singles(k, x), lambda x, k=k: two_steps(b[k], b[k + 1], x), x
                )
            return lax.cond(ends, lambda x: x + inbox[pl.ds(first, records), :], lambda x: x, x)

        return lax.switch(
            jnp.where(seen, 2, 0) + jnp.where(own, 1, 0), (plain, plain_own, seen_other, seen_own), x
        )

    x = jnp.broadcast_to(start[...], (records, states))
    per = steps // 4
    x = lax.fori_loop(0, per * (me + 1), filter_quad, x)
    outs = [
        pltpu.make_async_copy(a, b, out_sem.at[i])
        for i, (a, b) in enumerate(((filtered, filtered_far), (smoothed, smoothed_far)))
    ]
    outs[0].start()
    lax.fori_loop(per * (me + 1), per * devices, filter_quad, x)

    def smooth_quad(quad, r):
        block, t, b, m = regimes(quad)
        starts = packed(block) & (t == 0)
        seen = (m[0] + m[1] + m[2] + m[3] > 0) | starts

        def plain(r):
            if quads:
                return rows_product(r, quads[0][quad], quads[1][quad])
            return back_two(b[1], b[0], back_two(b[3], b[2], r))

        def added(k, r):
            return lax.cond(m[k] > 0, lambda r: r + delta[quad * 4 + k], lambda r: r, r)

        def stepped(r):
            for k in (2, 0):
                r = lax.cond(
                    m[k + 1] > 0,
                    lambda r, k=k: back(b[k], added(k + 1, back(b[k + 1], r))),
                    lambda r, k=k: back_two(b[k + 1], b[k], r),
                    r,
                )
                r = added(k, r)
            first = place(lax.bitwise_xor(block, me)) * rows + records
            return lax.cond(starts, lambda r: r + inbox[pl.ds(pl.multiple_of(first, 8), records), :], lambda r: r, r)

        return lax.cond(seen, stepped, plain, r)

    r = lax.fori_loop(
        0, per * (devices - 1 - me), lambda i, r: smooth_quad(devices * per - 1 - i, r), jnp.zeros((records, states), F32)
    )

    def smooth_own(i, r):
        quad = me * per + per - 1 - i
        block, t, b, m = regimes(quad)
        for k in (3, 2, 1, 0):
            e = back(b[k], r)
            smoothed[t + k] = filtered[t + k] + e
            r = lax.cond(m[k] > 0, lambda e, k=k: e + delta[quad * 4 + k], lambda e: e, e)
        return r

    def smooth_own_plain(r):
        own = [regimes(me * per + q) for q in range(per)]
        after, thirds = [None] * per, [None] * per
        for q in reversed(range(per)):
            _, t, b, _ = own[q]
            after[q], thirds[q] = r, back_two(b[3], b[2], r)
            r = rows_product(r, quads[0][me * per + q], quads[1][me * per + q]) if quads else back_two(b[1], b[0], thirds[q])
            smoothed[t] = filtered[t] + r
        for q in reversed(range(per)):
            _, t, b, _ = own[q]
            for k, e in ((1, back(b[1], thirds[q])), (2, thirds[q]), (3, back(b[3], after[q]))):
                smoothed[t + k] = filtered[t + k] + e
        return r

    lax.cond(table[me, COUNT_AT] > 0, lambda r: lax.fori_loop(0, per, smooth_own, r), smooth_own_plain, r)
    outs[1].start()
    for copy in outs:
        copy.wait()


def whole(memory=pltpu.VMEM):
    return pl.BlockSpec(memory_space=memory)


def xor_round(held, low, width, devices):
    return [held] + [
        lax.ppermute(held, "tm", [(i, i ^ (k << low)) for i in range(devices)]) for k in range(1, 1 << width)
    ]


def shards(observations, band_index, obs_mask, diffusivity, gain, back, initial_mean):
    steps, records, states = observations.shape
    bands = diffusivity.shape[0]
    devices = lax.axis_size("tm")
    rows = SLOTS * records + META
    params = pltpu.CompilerParams(vmem_limit_bytes=VMEM_BYTES)
    shape = jax.ShapeDtypeStruct
    message = pl.pallas_call(
        functools.partial(pack_kernel, bands),
        out_shape=shape((rows, states), F32),
        in_specs=[whole(pltpu.HBM)] * 6,
        out_specs=whole(),
        scratch_shapes=[
            pltpu.SMEM((steps,), jnp.int32),
            pltpu.SMEM((steps,), jnp.int32),
            pltpu.VMEM((steps, records, states), F32),
            pltpu.VMEM((bands, states), F32),
            pltpu.VMEM((bands, 8, states), F32),
            pltpu.VMEM((bands, states, states), F32),
            pltpu.VMEM((bands, states, states), F32),
            pltpu.VMEM((steps, records, states), F32),
            pltpu.SemaphoreType.DMA((4,)),
        ],
        compiler_params=pltpu.CompilerParams(vmem_limit_bytes=PACK_VMEM_BYTES),
        name="pack_message",
    )(band_index, obs_mask, observations, diffusivity, gain, back)
    matrix = lambda count: shape((count, states, states), BF)
    cost = lambda flops: pl.CostEstimate(flops=flops, bytes_accessed=4 * 2**20, transcendentals=0)

    def make_tables():
        return pl.pallas_call(
            functools.partial(tables_kernel, bands),
            out_shape=[shape((bands, 8, states), F32), shape((bands * bands, 16, states), F32)] + [matrix(bands)] * 4,
            in_specs=[whole()] * 3,
            out_specs=[whole()] * 6,
            compiler_params=params,
            cost_estimate=cost(2**28),
            name="tables",
        )(diffusivity, gain, back)

    def make_pairs(back_high, back_low):
        return pl.pallas_call(
            functools.partial(pairs_kernel, bands),
            out_shape=[matrix(bands * bands)] * 2,
            in_specs=[whole()] * 2,
            out_specs=[whole()] * 2,
            compiler_params=params,
            cost_estimate=cost(6 * bands**2 * states**3),
            name="pairs",
        )(back_high, back_low)

    bits = devices.bit_length() - 1
    pieces, fields, low, tables = [message], [], bits, None
    for width in [1] * (bits % 2) + [2] * (bits // 2):
        low -= width
        held = jnp.concatenate(pieces, 0)
        if fields and tables is None:
            tables = make_tables()
            held, tables = lax.optimization_barrier((held, tables))
        pieces = xor_round(held, low, width, devices)
        fields = [(low, 1 << width)] + fields
    tables = make_tables() if tables is None else tables
    tables = [*tables, *make_pairs(*tables[4:6])]
    out = shape((steps, records, states), F32)
    quads = devices * steps // 4
    deep = quads * states * states * 4 <= QUADS_BYTES
    return pl.pallas_call(
        functools.partial(main_kernel, bands, devices, fields, len(pieces)),
        out_shape=[out, out],
        in_specs=[whole()] * (2 + len(pieces) + len(tables)),
        out_specs=[whole(pltpu.HBM)] * 2,
        scratch_shapes=[
            pltpu.VMEM((steps, records, states), F32),
            pltpu.VMEM((steps, records, states), F32),
            pltpu.SemaphoreType.DMA((2,)),
            pltpu.VMEM((devices * rows, states), F32),
            pltpu.VMEM((devices, states), jnp.int32),
            pltpu.SMEM((devices, states), jnp.int32),
            pltpu.VMEM((devices * steps, records, states), F32),
            pltpu.SemaphoreType.DMA,
        ]
        + [pltpu.VMEM((quads, states, states), BF)] * (2 * deep),
        compiler_params=params,
        name="filter_and_smooth",
    )(observations, initial_mean[None, :], *pieces, *tables)


def solution(mesh):
    return jax.shard_map(
        shards,
        mesh=mesh,
        in_specs=(P("tm", "col", None), P("tm"), P("tm"), P(), P(), P(), P()),
        out_specs=(P("tm", "col", None), P("tm", "col", None)),
        check_vma=False,
    )
```

```python
import functools

import jax
import jax.numpy as jnp
from jax import lax
from jax.experimental import pallas as pl
from jax.experimental.pallas import tpu as pltpu
from jax.sharding import PartitionSpec as P

GRID = 16
SLOTS = 3
META = 8
BF, F32 = jnp.bfloat16, jnp.float32
VMEM_BYTES = 40 * 2**20
QUADS_BYTES = 2**24
PACK_VMEM_BYTES = 60 * 2**20


def lanes(steps):
    at, places = 0, []
    for size in (steps, steps, steps, steps // 2, steps // 4, steps // 4, steps // 8, steps // 8, 1):
        places.append(at)
        at += size
    return places


def halves(value):
    high = value.astype(BF)
    return high, (value - high.astype(F32)).astype(BF)


def dot(a, b):
    return jnp.dot(a, b, preferred_element_type=F32)


def rows_product(rows, high, low):
    m = rows.shape[0]
    rows_high, rows_low = halves(rows)
    both = dot(jnp.concatenate([rows_high, rows_low], 0), high)
    return both[:m] + both[m:] + dot(rows_high, low)


def from_cell(value, shift):
    cells = value.shape[-1]
    return pltpu.roll(value, (-shift) % cells, 1) if shift % cells else value


SHIFTS = (0, 1, -1, GRID, -GRID)


def stencils(diffusivity):
    cell = lax.broadcasted_iota(jnp.int32, diffusivity.shape, 1)
    cells = diffusivity.shape[1]
    row, column = cell // GRID, cell % GRID
    inside = {1: column < GRID - 1, -1: column > 0, GRID: row < cells // GRID - 1, -GRID: row > 0}
    parts = {
        s: jnp.where(inside[s], 0.5 * (diffusivity + from_cell(diffusivity, s)), 0.0)
        for s in SHIFTS[1:]
    }
    parts[0] = 1.0 - (parts[1] + parts[-1] + parts[GRID] + parts[-GRID])
    return parts


def two_step_shifts():
    return sorted({a + b for a in SHIFTS for b in SHIFTS}, key=abs)


def tree_sum(terms):
    while len(terms) > 1:
        terms = [sum(terms[i + 1 : i + 2], terms[i]) for i in range(0, len(terms), 2)]
    return terms[0]


def apply_stencil(weights, shifts, value):
    return tree_sum([weights[k : k + 1] * from_cell(value, s) for k, s in enumerate(shifts)])


def tables_kernel(bands, diffusivity, gain, back, one, two, gain_high, gain_low, back_high, back_low):
    first = stencils(diffusivity[...])
    for b in range(bands):
        for k, s in enumerate(SHIFTS):
            one[b, k : k + 1, :] = first[s][b : b + 1]
    for b in range(bands):
        for c in range(bands):
            total = {}
            for s in SHIFTS:
                for r in SHIFTS:
                    term = first[s][c : c + 1] * from_cell(first[r][b : b + 1], s)
                    total[s + r] = total[s + r] + term if s + r in total else term
            for k, s in enumerate(two_step_shifts()):
                two[b * bands + c, k : k + 1, :] = total[s]
    for b in range(bands):
        gain_high[b], gain_low[b] = halves(gain[b].T)
        back_high[b], back_low[b] = halves(back[b].T)


def pairs_kernel(bands, back_high, back_low, pair_high, pair_low):
    def pair(i, carry):
        earlier, later = i // bands, i % bands
        high, low = back_high[later], back_low[later]
        product = dot(high, back_high[earlier]) + (dot(low, back_high[earlier]) + dot(high, back_low[earlier]))
        pair_high[i], pair_low[i] = halves(product)
        return carry

    lax.fori_loop(0, bands * bands, pair, 0, unroll=4)


def pack_kernel(
    bands, band_far, mask_far, observations_far, diffusivity_far, gain, back, message, band, mask, observations, diffusivity, one,
    gain_here, back_here, delta, sem,
):
    steps, records, states = observations.shape
    near = (band, mask, observations, diffusivity)
    copies = [
        pltpu.make_async_copy(a, b, sem.at[i])
        for i, (a, b) in enumerate(zip((band_far, mask_far, observations_far, diffusivity_far), near))
    ]
    for copy in copies:
        copy.start()
    for copy in copies:
        copy.wait()
    lane = lax.broadcasted_iota(jnp.int32, (META, states), 1)
    meta = jnp.zeros((META, states), jnp.int32)
    band_at, mask_at, slot_at, pair_at, quad_at, quad_own_at, oct_at, oct_own_at, count_at = lanes(steps)

    def put(at, value):
        return jnp.where(lane == at, value, meta)

    count = jnp.int32(0)
    for t in range(steps):
        meta = put(band_at + t, band[t])
        meta = put(mask_at + t, mask[t])
        meta = put(slot_at + t, count)

        @pl.when((mask[t] > 0) & (count < SLOTS))
        def _(t=t, at=count):
            message[pl.ds(at * records, records), :] = observations[t]

        count = count + mask[t]
    packed = count > SLOTS
    for p in range(steps // 2):
        meta = put(pair_at + p, band[2 * p] * bands + band[2 * p + 1])
    ways, ways_own = [], []
    for q in range(steps // 4):
        m = [mask[4 * q + k] for k in range(4)]
        seen = m[0] + m[1] + m[2] + m[3]
        way = jnp.where(seen == 1, 2 + m[1] + 2 * m[2] + 3 * m[3], jnp.where(seen > 1, 1, 0))
        ways_own.append(way)
        ways.append(jnp.where(packed & ((seen > 0) | (q in (0, steps // 4 - 1))), 1, way))
        meta = put(quad_at + q, ways[q])
        meta = put(quad_own_at + q, way)
    for o in range(steps // 8):
        meta = put(oct_at + o, ways[2 * o] + ways[2 * o + 1])
        meta = put(oct_own_at + o, ways_own[2 * o] + ways_own[2 * o + 1])
    meta = put(count_at, count)
    message[SLOTS * records :, :] = meta.astype(F32)

    for slot in range(SLOTS):

        @pl.when(count <= slot)
        def _(slot=slot):
            message[slot * records : (slot + 1) * records, :] = jnp.zeros((records, states), F32)

    @pl.when(packed)
    def _():
        copies = [pltpu.make_async_copy(a, b, sem.at[i]) for i, (a, b) in enumerate(((gain, gain_here), (back, back_here)))]
        for copy in copies:
            copy.start()
        first = stencils(diffusivity[...])
        for b in range(bands):
            for k, s in enumerate(SHIFTS):
                one[b, k : k + 1, :] = first[s][b : b + 1]
        for copy in copies:
            copy.wait()

        def times(rows, matrix):
            return lax.dot_general(
                rows, matrix, (((1,), (1,)), ((), ())), precision=lax.Precision.HIGHEST, preferred_element_type=F32
            )

        def forward(t, x):
            p = apply_stencil(one[band[t]], SHIFTS, x)
            delta[t] = mask[t].astype(F32) * times(observations[t] - p, gain_here[band[t]])
            return p + delta[t]

        zeros = jnp.zeros((records, states), F32)
        message[0:records, :] = lax.fori_loop(0, steps, forward, zeros)

        def backward(i, r):
            t = steps - 1 - i
            return times(r, back_here[band[t]]) + delta[t]

        message[records : 2 * records, :] = lax.fori_loop(0, steps, backward, zeros)


def main_kernel(
    bands,
    devices,
    fields,
    pieces,
    observations,
    start,
    *refs,
):
    parts, refs = refs[:pieces], refs[pieces:]
    (one, two, gain_high, gain_low, back_high, back_low, pair_high, pair_low), refs = refs[:8], refs[8:]
    (filtered_far, smoothed_far, held, smoothed, out_sem), refs = refs[:5], refs[5:]
    (inbox, meta, table, delta, pushed, sem), quads = refs[:6], refs[6:]
    steps, records, states = observations.shape
    per = steps // 4
    rows = parts[0].shape[0] // (devices // pieces)
    me = lax.axis_index("tm")

    def place(apart):
        found, scale = jnp.int32(0), 1
        for shift, width in reversed(fields):
            found = found + lax.bitwise_and(lax.shift_right_logical(apart, shift), width - 1) * scale
            scale *= width
        return found

    def apart_at(position):
        apart, position = 0, int(position)
        for shift, width in reversed(fields):
            apart |= (position % width) << shift
            position //= width
        return apart

    each = parts[0].shape[0]
    for k in range(devices):
        at = k * rows + SLOTS * records - k * rows // each * each
        block = lax.bitwise_xor(me, apart_at(k))
        meta[pl.ds(block, 1), :] = parts[k * rows // each][at : at + 1, :].astype(jnp.int32)
    copy = pltpu.make_async_copy(meta, table, sem)
    copy.start()
    for i, part in enumerate(parts):
        inbox[i * each : (i + 1) * each, :] = part[...]
    copy.wait()

    def step(b, x):
        return apply_stencil(one[b], SHIFTS, x)

    def two_steps(pair, x):
        return apply_stencil(two[pair], two_step_shifts(), x)

    def innovation(b, difference):
        return rows_product(difference, gain_high[b], gain_low[b])

    def back(b, r):
        return rows_product(r, back_high[b], back_low[b])

    def back_two(pair, r):
        return rows_product(r, pair_high[pair], pair_low[pair])

    band_at, mask_at, slot_at, pair_at, quad_at, quad_own_at, oct_at, oct_own_at, count_at = lanes(steps)

    def pairs(block, q):
        return table[block, pair_at + 2 * q], table[block, pair_at + 2 * q + 1]

    def four(at, block, q):
        return [table[block, at + 4 * q + k] for k in range(4)]

    def prepare(block, q):
        if quads:
            right, left = pairs(block, q)
            high, low = pair_high[left], pair_low[left]
            product = dot(high, pair_high[right]) + (dot(low, pair_high[right]) + dot(high, pair_low[right]))
            quads[0][block * per + q], quads[1][block * per + q] = halves(product)

    def over_quad(block, q, r):
        if quads:
            return rows_product(r, quads[0][block * per + q], quads[1][block * per + q])
        early, late = pairs(block, q)
        return back_two(early, back_two(late, r))

    def added(seen, at, r):
        return jnp.where(seen > 0, r + delta[at], r)

    def plain(block, q, x):
        early, late = pairs(block, q)
        at = (block * per + q) * 4 + 1
        prepare(block, q)
        pushed[block * per + q] = jnp.zeros_like(x)
        x = two_steps(early, x)
        held[at + 1] = x
        x = two_steps(late, x)
        held[at + 3] = x
        return x

    def filter_quad(block, q, x):
        at = (block * per + q) * 4
        own = block == me
        first = pl.multiple_of(place(lax.bitwise_xor(block, me)) * rows, 8)

        def keep(k, x):
            held[at + k + 1] = x
            return x

        def corrected(b, k, p, packed=False):
            slot = lax.rem(table[block, slot_at + 4 * q + k], SLOTS)
            sent = inbox[pl.ds(pl.multiple_of(first + slot * records, 8), records), :]
            y = jnp.where(packed, 0.0, jnp.where(own, observations[4 * q + k], sent))
            change = innovation(b, y - p)
            delta[at + k] = change
            return change

        def one_seen(k, x):
            b = four(band_at, block, q)
            early, late = pairs(block, q)
            prepare(block, q)
            if k >= 2:
                x = keep(1, two_steps(early, x))
            if k % 2:
                x = keep(k - 1, step(b[k - 1], x))
            p = step(b[k], x)
            change = corrected(b[k], k, p)
            x = keep(k, p + change)
            if k % 2 == 0:
                x = keep(k + 1, step(b[k + 1], x))
            if k < 2:
                x = keep(3, two_steps(late, x))
            if k == 0:
                change = jnp.zeros_like(x)
            elif k == 1:
                change = back(b[0], change)
            else:
                change = back_two(early, change if k == 2 else back(b[2], change))
            pushed[block * per + q] = change
            return x

        def any_seen(x):
            b, m = four(band_at, block, q), four(mask_at, block, q)
            packed = (table[block, count_at] > SLOTS) & jnp.logical_not(own)
            prepare(block, q)
            for k in range(4):
                p = step(b[k], x)
                x = keep(k, lax.cond(m[k] > 0, lambda p, k=k: p + corrected(b[k], k, p, packed), lambda p: p, p))
            r = jnp.zeros_like(x)
            for k in (3, 2, 1):
                r = back(b[k - 1], added(m[k], at + k, r))
            r_sent = inbox[pl.ds(pl.multiple_of(first + records, 8), records), :]
            pushed[block * per + q] = jnp.where(packed & (q == 0), r + r_sent, r)
            return keep(3, jnp.where(packed & (q == per - 1), x + inbox[pl.ds(first, records), :], x))

        return lax.switch(
            table[block, jnp.where(own, quad_own_at, quad_at) + q],
            [functools.partial(plain, block, q), any_seen] + [functools.partial(one_seen, k) for k in range(4)],
            x,
        )

    def filter_oct(block, o, x):
        return lax.cond(
            table[block, jnp.where(block == me, oct_own_at, oct_at) + o] == 0,
            lambda x: plain(block, 2 * o + 1, plain(block, 2 * o, x)),
            lambda x: lax.fori_loop(2 * o, 2 * o + 2, functools.partial(filter_quad, block), x),
            x,
        )

    def filter_block(block, x):
        return lax.fori_loop(0, per // 2, functools.partial(filter_oct, block), x)

    held[0] = jnp.broadcast_to(start[...], (records, states))
    x = lax.fori_loop(0, me + 1, filter_block, held[0])
    own_bands = [four(band_at, me, q) for q in range(per)]
    own_masks = [four(mask_at, me, q) for q in range(per)]
    for q in range(per):
        for k in (0, 2):
            at = me * steps + q * 4 + k
            seen = own_masks[q][k] + own_masks[q][k + 1] > 0
            held[at + 1] = jnp.where(seen, held[at + 1], step(own_bands[q][k], held[at]))
    outs = [
        pltpu.make_async_copy(a, b, out_sem.at[i])
        for i, (a, b) in enumerate(((held.at[pl.ds(me * steps + 1, steps)], filtered_far), (smoothed, smoothed_far)))
    ]
    outs[0].start()
    lax.fori_loop(me + 1, devices, filter_block, x)

    def smooth_block(i, r):
        block = devices - 1 - i
        for q in reversed(range(per)):
            r = over_quad(block, q, r) + pushed[block * per + q]
            r = added(table[block, mask_at + 4 * q], block * steps + 4 * q, r)
        return r

    r = lax.fori_loop(0, devices - 1 - me, smooth_block, jnp.zeros((records, states), F32))

    def smooth(q, k, e):
        smoothed[q * 4 + k] = held[me * steps + q * 4 + k + 1] + e
        return added(own_masks[q][k], me * steps + q * 4 + k, e)

    after = [None] * per
    for q in reversed(range(per)):
        after[q] = r
        r = smooth(q, 0, over_quad(me, q, r) + pushed[me * per + q])
    for k in (3, 2, 1):
        for q in range(per):
            after[q] = smooth(q, k, back(own_bands[q][k], after[q]))
    outs[1].start()
    for copy in outs:
        copy.wait()


def whole(memory=pltpu.VMEM):
    return pl.BlockSpec(memory_space=memory)


def xor_round(held, low, width, devices):
    return [held] + [
        lax.ppermute(held, "tm", [(i, i ^ (k << low)) for i in range(devices)]) for k in range(1, 1 << width)
    ]


def shards(observations, band_index, obs_mask, diffusivity, gain, back, initial_mean):
    steps, records, states = observations.shape
    bands = diffusivity.shape[0]
    devices = lax.axis_size("tm")
    rows = SLOTS * records + META
    params = pltpu.CompilerParams(vmem_limit_bytes=VMEM_BYTES)
    shape = jax.ShapeDtypeStruct
    message = pl.pallas_call(
        functools.partial(pack_kernel, bands),
        out_shape=shape((rows, states), F32),
        in_specs=[whole(pltpu.HBM)] * 6,
        out_specs=whole(),
        scratch_shapes=[
            pltpu.SMEM((steps,), jnp.int32),
            pltpu.SMEM((steps,), jnp.int32),
            pltpu.VMEM((steps, records, states), F32),
            pltpu.VMEM((bands, states), F32),
            pltpu.VMEM((bands, 8, states), F32),
            pltpu.VMEM((bands, states, states), F32),
            pltpu.VMEM((bands, states, states), F32),
            pltpu.VMEM((steps, records, states), F32),
            pltpu.SemaphoreType.DMA((4,)),
        ],
        compiler_params=pltpu.CompilerParams(vmem_limit_bytes=PACK_VMEM_BYTES),
        name="pack_message",
    )(band_index, obs_mask, observations, diffusivity, gain, back)
    matrix = lambda count: shape((count, states, states), BF)
    cost = lambda flops: pl.CostEstimate(flops=flops, bytes_accessed=4 * 2**20, transcendentals=0)

    def make_tables():
        return pl.pallas_call(
            functools.partial(tables_kernel, bands),
            out_shape=[shape((bands, 8, states), F32), shape((bands * bands, 16, states), F32)] + [matrix(bands)] * 4,
            in_specs=[whole()] * 3,
            out_specs=[whole()] * 6,
            compiler_params=params,
            cost_estimate=cost(2**28),
            name="tables",
        )(diffusivity, gain, back)

    def make_pairs(back_high, back_low):
        return pl.pallas_call(
            functools.partial(pairs_kernel, bands),
            out_shape=[matrix(bands * bands)] * 2,
            in_specs=[whole()] * 2,
            out_specs=[whole()] * 2,
            compiler_params=params,
            cost_estimate=cost(6 * bands**2 * states**3),
            name="pairs",
        )(back_high, back_low)

    bits = devices.bit_length() - 1
    pieces, fields, low, tables = [message], [], bits, None
    for width in [1] * (bits % 2) + [2] * (bits // 2):
        low -= width
        held = jnp.concatenate(pieces, 0)
        if fields and tables is None:
            tables = make_tables()
            held, tables = lax.optimization_barrier((held, tables))
        pieces = xor_round(held, low, width, devices)
        fields = [(low, 1 << width)] + fields
    tables = make_tables() if tables is None else tables
    tables = [*tables, *make_pairs(*tables[4:6])]
    out = shape((steps, records, states), F32)
    quads = devices * steps // 4
    deep = quads * states * states * 4 <= QUADS_BYTES
    return pl.pallas_call(
        functools.partial(main_kernel, bands, devices, fields, len(pieces)),
        out_shape=[out, out],
        in_specs=[whole()] * (2 + len(pieces) + len(tables)),
        out_specs=[whole(pltpu.HBM)] * 2,
        scratch_shapes=[
            pltpu.VMEM((devices * steps + 1, records, states), F32),
            pltpu.VMEM((steps, records, states), F32),
            pltpu.SemaphoreType.DMA((2,)),
            pltpu.VMEM((devices * rows, states), F32),
            pltpu.VMEM((devices, states), jnp.int32),
            pltpu.SMEM((devices, states), jnp.int32),
            pltpu.VMEM((devices * steps, records, states), F32),
            pltpu.VMEM((quads, records, states), F32),
            pltpu.SemaphoreType.DMA,
        ]
        + [pltpu.VMEM((quads, states, states), BF)] * (2 * deep),
        compiler_params=params,
        name="filter_and_smooth",
    )(observations, initial_mean[None, :], *pieces, *tables)


def solution(mesh):
    return jax.shard_map(
        shards,
        mesh=mesh,
        in_specs=(P("tm", "col", None), P("tm"), P("tm"), P(), P(), P(), P()),
        out_specs=(P("tm", "col", None), P("tm", "col", None)),
        check_vma=False,
    )
```

```python
import functools

import jax
import jax.numpy as jnp
from jax import lax
from jax.experimental import pallas as pl
from jax.experimental.pallas import tpu as pltpu
from jax.sharding import PartitionSpec as P

GRID = 16
SLOTS = 3
META = 8
BF, F32 = jnp.bfloat16, jnp.float32
VMEM_BYTES = 44 * 2**20
QUADS_BYTES = 2**24
PACK_VMEM_BYTES = 60 * 2**20


def lanes(steps):
    at, places = 0, []
    for size in (steps, steps, steps, steps // 2, steps // 4, steps // 4, steps // 8, steps // 8, 1):
        places.append(at)
        at += size
    return places


def halves(value):
    high = value.astype(BF)
    return high, (value - high.astype(F32)).astype(BF)


def dot(a, b):
    return jnp.dot(a, b, preferred_element_type=F32)


def rows_product(rows, high, low):
    m = rows.shape[0]
    rows_high, rows_low = halves(rows)
    both = dot(jnp.concatenate([rows_high, rows_low], 0), high)
    return both[:m] + both[m:] + dot(rows_high, low)


def from_cell(value, shift):
    cells = value.shape[-1]
    return pltpu.roll(value, (-shift) % cells, 1) if shift % cells else value


SHIFTS = (0, 1, -1, GRID, -GRID)


def stencils(diffusivity):
    cell = lax.broadcasted_iota(jnp.int32, diffusivity.shape, 1)
    cells = diffusivity.shape[1]
    row, column = cell // GRID, cell % GRID
    inside = {1: column < GRID - 1, -1: column > 0, GRID: row < cells // GRID - 1, -GRID: row > 0}
    parts = {
        s: jnp.where(inside[s], 0.5 * (diffusivity + from_cell(diffusivity, s)), 0.0)
        for s in SHIFTS[1:]
    }
    parts[0] = 1.0 - (parts[1] + parts[-1] + parts[GRID] + parts[-GRID])
    return parts


def two_step_shifts():
    return sorted({a + b for a in SHIFTS for b in SHIFTS}, key=abs)


def tree_sum(terms):
    while len(terms) > 1:
        terms = [sum(terms[i + 1 : i + 2], terms[i]) for i in range(0, len(terms), 2)]
    return terms[0]


def apply_stencil(weights, shifts, value):
    return tree_sum([weights[k : k + 1] * from_cell(value, s) for k, s in enumerate(shifts)])


def folded_lane(cells, lane):
    half, rest = lane // (cells // 2), lax.rem(lane, cells // 2)
    return rest // (GRID // 2) * GRID + lax.rem(rest, GRID // 2) * 2 + half


def apply_folded(weights, shifts, value):
    half = value.shape[1] // 2
    parts, rolled = (value[:, :half], value[:, half:]), {}

    def moved(part, by):
        if (part, by) not in rolled:
            rolled[part, by] = from_cell(parts[part], by)
        return rolled[part, by]

    out = []
    for h in (0, 1):
        terms = []
        for k, s in enumerate(shifts):
            down = (s + GRID // 2) // GRID
            across = h + s - down * GRID
            terms.append(weights[k : k + 1, h * half : (h + 1) * half] * moved(across % 2, down * (GRID // 2) + across // 2))
        out.append(tree_sum(terms))
    return jnp.concatenate(out, 1)


def reorder(rows, order):
    high = rows.astype(BF)
    rest = rows - high.astype(F32)
    middle = rest.astype(BF)
    low = (rest - middle.astype(F32)).astype(BF)
    return dot(high, order) + (dot(middle, order) + dot(low, order))


def folded_rows(value, space):
    cells = value.shape[0]
    starts = [r * GRID + h for h in (0, 1) for r in range(cells // GRID)]
    columns = []
    for i in range(space.shape[0]):
        space[i] = value[:, i * 128 : (i + 1) * 128]
        columns.append(jnp.concatenate([space[i, pl.ds(at, GRID // 2, stride=2), :] for at in starts], 0))
    return jnp.concatenate(columns, 1)


def tables_kernel(
    bands, diffusivity, gain, back, start, one, two, gain_high, gain_low, next_high, next_low, back_high, back_low, fold, unfold,
    first_rows, space, natural,
):
    cells = diffusivity.shape[1]
    index = [lax.broadcasted_iota(jnp.int32, (cells, cells), d) for d in (0, 1)]
    fold[...] = (index[0] == folded_lane(cells, index[1])).astype(F32).astype(BF)
    unfold[...] = (index[1] == folded_lane(cells, index[0])).astype(F32).astype(BF)
    unit = (index[0] == index[1]).astype(F32)
    first = stencils(diffusivity[...])
    natural[...] = jnp.zeros(natural.shape, F32)
    for b in range(bands):
        for k, s in enumerate(SHIFTS):
            natural[b * 8 + k : b * 8 + k + 1, :] = first[s][b : b + 1]
    own_rows = bands * 8
    for b in range(bands):
        for c in range(bands):
            total = {}
            for s in SHIFTS:
                for r in SHIFTS:
                    term = first[s][c : c + 1] * from_cell(first[r][b : b + 1], s)
                    total[s + r] = total[s + r] + term if s + r in total else term
            for k, s in enumerate(two_step_shifts()):
                at = own_rows + (b * bands + c) * 16 + k
                natural[at : at + 1, :] = total[s]
    at = own_rows + bands * bands * 16
    natural[at : at + 1, :] = start[...]
    folded = reorder(natural[...], fold[...])
    one[...] = folded[:own_rows].reshape(one.shape)
    two[...] = folded[own_rows:at].reshape(two.shape)
    first_rows[...] = jnp.broadcast_to(folded[at : at + 1], first_rows.shape)
    for b in range(bands):
        weights = natural[b * 8 : b * 8 + 8, :]
        gain_high[b], gain_low[b] = halves(folded_rows(gain[b], space.at[b, 0]).T)
        after = apply_stencil(weights, SHIFTS, unit - gain[b])
        after = folded_rows(after, space.at[b, 1]).T
        next_high[b], next_low[b] = halves(folded_rows(after, space.at[b, 2]))
        after = folded_rows(back[b], space.at[b, 3]).T
        back_high[b], back_low[b] = halves(folded_rows(after, space.at[b, 4]))


def pairs_kernel(bands, back_high, back_low, pair_high, pair_low):
    def pair(i, carry):
        earlier, later = i // bands, i % bands
        high, low = back_high[later], back_low[later]
        product = dot(high, back_high[earlier]) + (dot(low, back_high[earlier]) + dot(high, back_low[earlier]))
        pair_high[i], pair_low[i] = halves(product)
        return carry

    lax.fori_loop(0, bands * bands, pair, 0, unroll=4)


def pack_kernel(
    bands, band_far, mask_far, observations_far, diffusivity_far, gain, back, message, band, mask, observations, diffusivity, one,
    gain_here, back_here, delta, sem,
):
    steps, records, states = observations.shape
    near = (band, mask, observations, diffusivity)
    copies = [
        pltpu.make_async_copy(a, b, sem.at[i])
        for i, (a, b) in enumerate(zip((band_far, mask_far, observations_far, diffusivity_far), near))
    ]
    for copy in copies:
        copy.start()
    for copy in copies[:2]:
        copy.wait()
    lane = lax.broadcasted_iota(jnp.int32, (META, states), 1)
    meta = jnp.zeros((META, states), jnp.int32)
    band_at, mask_at, slot_at, pair_at, quad_at, quad_own_at, oct_at, oct_own_at, count_at = lanes(steps)

    def put(at, value):
        return jnp.where(lane == at, value, meta)

    count = jnp.int32(0)
    for t in range(steps):
        meta = put(band_at + t, band[t])
        meta = put(mask_at + t, mask[t])
        meta = put(slot_at + t, count)
        count = count + mask[t]
    packed = count > SLOTS
    for p in range(steps // 2):
        meta = put(pair_at + p, band[2 * p] * bands + band[2 * p + 1])
    ways, ways_own = [], []
    for q in range(steps // 4):
        m = [mask[4 * q + k] for k in range(4)]
        seen = m[0] + m[1] + m[2] + m[3]
        way = jnp.where(seen == 1, 2 + m[1] + 2 * m[2] + 3 * m[3], jnp.where(seen > 1, 1, 0))
        ways_own.append(way)
        ways.append(jnp.where(packed & ((seen > 0) | (q in (0, steps // 4 - 1))), 1, way))
        meta = put(quad_at + q, ways[q])
        meta = put(quad_own_at + q, way)
    for o in range(steps // 8):
        meta = put(oct_at + o, ways[2 * o] + ways[2 * o + 1])
        meta = put(oct_own_at + o, ways_own[2 * o] + ways_own[2 * o + 1])
    meta = put(count_at, count)
    message[SLOTS * records :, :] = meta.astype(F32)
    for copy in copies[2:]:
        copy.wait()
    at = jnp.int32(0)
    for t in range(steps):

        @pl.when((mask[t] > 0) & (at < SLOTS))
        def _(t=t, at=at):
            message[pl.ds(pl.multiple_of(at * records, 8), records), :] = observations[t]

        at = at + mask[t]

    for slot in range(SLOTS):

        @pl.when(count <= slot)
        def _(slot=slot):
            message[slot * records : (slot + 1) * records, :] = jnp.zeros((records, states), F32)

    @pl.when(packed)
    def _():
        copies = [pltpu.make_async_copy(a, b, sem.at[i]) for i, (a, b) in enumerate(((gain, gain_here), (back, back_here)))]
        for copy in copies:
            copy.start()
        first = stencils(diffusivity[...])
        for b in range(bands):
            for k, s in enumerate(SHIFTS):
                one[b, k : k + 1, :] = first[s][b : b + 1]
        for copy in copies:
            copy.wait()

        def times(rows, matrix):
            return lax.dot_general(
                rows, matrix, (((1,), (1,)), ((), ())), precision=lax.Precision.HIGHEST, preferred_element_type=F32
            )

        def forward(t, x):
            p = apply_stencil(one[band[t]], SHIFTS, x)
            delta[t] = mask[t].astype(F32) * times(observations[t] - p, gain_here[band[t]])
            return p + delta[t]

        zeros = jnp.zeros((records, states), F32)
        message[0:records, :] = lax.fori_loop(0, steps, forward, zeros)

        def backward(i, r):
            t = steps - 1 - i
            return times(r, back_here[band[t]]) + delta[t]

        message[records : 2 * records, :] = lax.fori_loop(0, steps, backward, zeros)


def main_kernel(
    bands,
    devices,
    fields,
    pieces,
    observations,
    *refs,
):
    parts, refs = refs[:pieces], refs[pieces:]
    (one, two, gain_high, gain_low, next_high, next_low, back_high, back_low, fold, unfold, first_rows), refs = refs[:11], refs[11:]
    (pair_high, pair_low, filtered_far, smoothed_far, held, outward, out_sem), refs = refs[:7], refs[7:]
    (inbox, meta, table, delta, pushed, sem), quads = refs[:6], refs[6:]
    steps, records, states = observations.shape
    per = steps // 4
    rows = parts[0].shape[0] // (devices // pieces)
    me = lax.axis_index("tm")

    def place(apart):
        found, scale = jnp.int32(0), 1
        for shift, width in reversed(fields):
            found = found + lax.bitwise_and(lax.shift_right_logical(apart, shift), width - 1) * scale
            scale *= width
        return found

    def apart_at(position):
        apart, position = 0, int(position)
        for shift, width in reversed(fields):
            apart |= (position % width) << shift
            position //= width
        return apart

    each = parts[0].shape[0]
    for k in range(devices):
        at = k * rows + SLOTS * records - k * rows // each * each
        block = lax.bitwise_xor(me, apart_at(k))
        meta[pl.ds(block, 1), :] = parts[k * rows // each][at : at + 1, :].astype(jnp.int32)
    copy = pltpu.make_async_copy(meta, table, sem)
    copy.start()
    for i, part in enumerate(parts):
        inbox[i * each : (i + 1) * each, :] = part[...]
    copy.wait()

    def step(b, x):
        return apply_folded(one[b], SHIFTS, x)

    def two_steps(pair, x):
        return apply_folded(two[pair], two_step_shifts(), x)

    def observed_step(b, x, y):
        return rows_product(x, next_high[b], next_low[b]) + rows_product(y, gain_high[b], gain_low[b])

    def back(b, r):
        return rows_product(r, back_high[b], back_low[b])

    def back_two(pair, r):
        return rows_product(r, pair_high[pair], pair_low[pair])

    band_at, mask_at, slot_at, pair_at, quad_at, quad_own_at, oct_at, oct_own_at, count_at = lanes(steps)

    def pairs(block, q):
        return table[block, pair_at + 2 * q], table[block, pair_at + 2 * q + 1]

    def four(at, block, q):
        return [table[block, at + 4 * q + k] for k in range(4)]

    def prepare(block, q):
        if quads:
            right, left = pairs(block, q)
            high, low = pair_high[left], pair_low[left]
            product = dot(high, pair_high[right]) + (dot(low, pair_high[right]) + dot(high, pair_low[right]))
            quads[0][block * per + q], quads[1][block * per + q] = halves(product)

    def over_quad(block, q, r):
        if quads:
            return rows_product(r, quads[0][block * per + q], quads[1][block * per + q])
        early, late = pairs(block, q)
        return back_two(early, back_two(late, r))

    def added(seen, at, r):
        return jnp.where(seen > 0, r + delta[at], r)

    def plain(block, q, x):
        early, late = pairs(block, q)
        at = (block * per + q) * 4 + 1
        prepare(block, q)
        pushed[block * per + q] = jnp.zeros_like(x)
        x = two_steps(early, x)
        held[at + 1] = x
        x = two_steps(late, x)
        held[at + 3] = x
        return x

    def filter_quad(block, q, x):
        at = (block * per + q) * 4
        own = block == me
        first = pl.multiple_of(place(lax.bitwise_xor(block, me)) * rows, 8)

        def keep(k, x):
            held[at + k + 1] = x
            return x

        def corrected(b, k, x, packed=False):
            slot = lax.rem(table[block, slot_at + 4 * q + k], SLOTS)
            sent = inbox[pl.ds(pl.multiple_of(first + slot * records, 8), records), :]
            y = jnp.where(packed, 0.0, jnp.where(own, observations[4 * q + k], sent))
            p, x = step(b, x), observed_step(b, x, y)
            delta[at + k] = x - p
            held[at + k + 1] = x
            return x

        def one_seen(k, x):
            b = four(band_at, block, q)
            early, late = pairs(block, q)
            prepare(block, q)
            if k >= 2:
                x = keep(1, two_steps(early, x))
            if k % 2:
                x = keep(k - 1, step(b[k - 1], x))
            x = corrected(b[k], k, x)
            change = delta[at + k]
            if k % 2 == 0:
                x = keep(k + 1, step(b[k + 1], x))
            if k < 2:
                x = keep(3, two_steps(late, x))
            if k == 0:
                change = jnp.zeros_like(x)
            elif k == 1:
                change = back(b[0], change)
            else:
                change = back_two(early, change if k == 2 else back(b[2], change))
            pushed[block * per + q] = change
            return x

        def any_seen(x):
            b, m = four(band_at, block, q), four(mask_at, block, q)
            packed = (table[block, count_at] > SLOTS) & jnp.logical_not(own)
            prepare(block, q)
            for k in range(4):
                x = lax.cond(
                    m[k] > 0,
                    lambda x, k=k: corrected(b[k], k, x, packed),
                    lambda x, k=k: keep(k, step(b[k], x)),
                    x,
                )
            r = jnp.zeros_like(x)
            for k in (3, 2, 1):
                r = back(b[k - 1], added(m[k], at + k, r))
            pushed[block * per + q] = r

            def add_sent(slot):
                sent = inbox[pl.ds(pl.multiple_of(first + slot * records, 8), records), :]
                return lambda x: x + reorder(sent, fold[...])

            pushed[block * per + q] = lax.cond(packed & (q == 0), add_sent(1), lambda r: r, r)
            return keep(3, lax.cond(packed & (q == per - 1), add_sent(0), lambda x: x, x))

        return lax.switch(
            table[block, jnp.where(own, quad_own_at, quad_at) + q],
            [functools.partial(plain, block, q), any_seen] + [functools.partial(one_seen, k) for k in range(4)],
            x,
        )

    def filter_oct(block, o, x):
        return lax.cond(
            table[block, jnp.where(block == me, oct_own_at, oct_at) + o] == 0,
            lambda x: plain(block, 2 * o + 1, plain(block, 2 * o, x)),
            lambda x: lax.fori_loop(2 * o, 2 * o + 2, functools.partial(filter_quad, block), x),
            x,
        )

    def filter_block(block, x):
        return lax.fori_loop(0, per // 2, functools.partial(filter_oct, block), x)

    held[0] = first_rows[...]
    x = lax.fori_loop(0, me + 1, filter_block, held[0])
    own_bands = [four(band_at, me, q) for q in range(per)]
    own_masks = [four(mask_at, me, q) for q in range(per)]
    for q in range(per):
        for k in (0, 2):
            at = me * steps + q * 4 + k
            seen = own_masks[q][k] + own_masks[q][k + 1] > 0
            held[at + 1] = jnp.where(seen, held[at + 1], step(own_bands[q][k], held[at]))
    outs = [
        [pltpu.make_async_copy(outward.at[k, i], far.at[:, k], out_sem.at[k, i]) for i, far in enumerate((filtered_far, smoothed_far))]
        for k in range(4)
    ]
    lax.fori_loop(me + 1, devices, filter_block, x)

    def smooth_block(i, r):
        block = devices - 1 - i
        for q in reversed(range(per)):
            r = over_quad(block, q, r) + pushed[block * per + q]
            r = added(table[block, mask_at + 4 * q], block * steps + 4 * q, r)
        return r

    r = lax.fori_loop(0, devices - 1 - me, smooth_block, jnp.zeros((records, states), F32))

    def leave(k, after):
        before = [held[me * steps + q * 4 + k + 1] for q in range(per)]
        rows_out = jnp.concatenate(before + [x + e for x, e in zip(before, after)], 0)
        outward[k] = reorder(rows_out, unfold[...]).reshape(outward.shape[1:])
        for copy in outs[k]:
            copy.start()
        return [added(own_masks[q][k], me * steps + q * 4 + k, after[q]) for q in range(per)]

    after, ends = [None] * per, [None] * per
    for q in reversed(range(per)):
        after[q] = r
        ends[q] = over_quad(me, q, r) + pushed[me * per + q]
        r = added(own_masks[q][0], me * steps + q * 4, ends[q])
    leave(0, ends)
    for k in (3, 2, 1):
        after = leave(k, [back(own_bands[q][k], after[q]) for q in range(per)])
    for copy in sum(outs, []):
        copy.wait()


def whole(memory=pltpu.VMEM):
    return pl.BlockSpec(memory_space=memory)


def xor_round(held, low, width, devices):
    return [held] + [
        lax.ppermute(held, "tm", [(i, i ^ (k << low)) for i in range(devices)]) for k in range(1, 1 << width)
    ]


def shards(observations, band_index, obs_mask, diffusivity, gain, back, initial_mean):
    steps, records, states = observations.shape
    bands = diffusivity.shape[0]
    devices = lax.axis_size("tm")
    rows = SLOTS * records + META
    params = pltpu.CompilerParams(vmem_limit_bytes=VMEM_BYTES)
    shape = jax.ShapeDtypeStruct
    message = pl.pallas_call(
        functools.partial(pack_kernel, bands),
        out_shape=shape((rows, states), F32),
        in_specs=[whole(pltpu.HBM)] * 6,
        out_specs=whole(),
        scratch_shapes=[
            pltpu.SMEM((steps,), jnp.int32),
            pltpu.SMEM((steps,), jnp.int32),
            pltpu.VMEM((steps, records, states), F32),
            pltpu.VMEM((bands, states), F32),
            pltpu.VMEM((bands, 8, states), F32),
            pltpu.VMEM((bands, states, states), F32),
            pltpu.VMEM((bands, states, states), F32),
            pltpu.VMEM((steps, records, states), F32),
            pltpu.SemaphoreType.DMA((4,)),
        ],
        compiler_params=pltpu.CompilerParams(vmem_limit_bytes=PACK_VMEM_BYTES),
        name="pack_message",
    )(band_index, obs_mask, observations, diffusivity, gain, back)
    matrix = lambda count: shape((count, states, states), BF)
    cost = lambda flops: pl.CostEstimate(flops=flops, bytes_accessed=4 * 2**20, transcendentals=0)

    def make_tables():
        return pl.pallas_call(
            functools.partial(tables_kernel, bands),
            out_shape=[shape((bands, 8, states), F32), shape((bands * bands, 16, states), F32)]
            + [matrix(bands)] * 6
            + [shape((states, states), BF)] * 2
            + [shape((records, states), F32)],
            in_specs=[whole()] * 4,
            out_specs=[whole()] * 11,
            scratch_shapes=[
                pltpu.VMEM((bands, 5, states // 128, states, 128), F32),
                pltpu.VMEM((bands * 8 + bands * bands * 16 + 8, states), F32),
            ],
            compiler_params=params,
            cost_estimate=cost(2**28),
            name="tables",
        )(diffusivity, gain, back, initial_mean[None, :])

    def make_pairs(back_high, back_low):
        return pl.pallas_call(
            functools.partial(pairs_kernel, bands),
            out_shape=[matrix(bands * bands)] * 2,
            in_specs=[whole()] * 2,
            out_specs=[whole()] * 2,
            compiler_params=params,
            cost_estimate=cost(6 * bands**2 * states**3),
            name="pairs",
        )(back_high, back_low)

    bits = devices.bit_length() - 1
    pieces, fields, low, tables = [message], [], bits, None
    for width in [1] * (bits % 2) + [2] * (bits // 2):
        low -= width
        held = jnp.concatenate(pieces, 0)
        if fields and tables is None:
            tables = make_tables()
            held, tables = lax.optimization_barrier((held, tables))
        pieces = xor_round(held, low, width, devices)
        fields = [(low, 1 << width)] + fields
    tables = make_tables() if tables is None else tables
    tables = [*tables, *make_pairs(*tables[6:8])]
    out = shape((steps // 4, 4, records, states), F32)
    quads = devices * steps // 4
    deep = quads * states * states * 4 <= QUADS_BYTES
    filtered, smoothed = pl.pallas_call(
        functools.partial(main_kernel, bands, devices, fields, len(pieces)),
        out_shape=[out, out],
        in_specs=[whole()] * (1 + len(pieces) + len(tables)),
        out_specs=[whole(pltpu.HBM)] * 2,
        scratch_shapes=[
            pltpu.VMEM((devices * steps + 1, records, states), F32),
            pltpu.VMEM((4, 2, steps // 4, records, states), F32),
            pltpu.SemaphoreType.DMA((4, 2)),
            pltpu.VMEM((devices * rows, states), F32),
            pltpu.VMEM((devices, states), jnp.int32),
            pltpu.SMEM((devices, states), jnp.int32),
            pltpu.VMEM((devices * steps, records, states), F32),
            pltpu.VMEM((quads, records, states), F32),
            pltpu.SemaphoreType.DMA,
        ]
        + [pltpu.VMEM((quads, states, states), BF)] * (2 * deep),
        compiler_params=params,
        name="filter_and_smooth",
    )(observations, *pieces, *tables)
    return filtered.reshape(observations.shape), smoothed.reshape(observations.shape)


def solution(mesh):
    return jax.shard_map(
        shards,
        mesh=mesh,
        in_specs=(P("tm", "col", None), P("tm"), P("tm"), P(), P(), P(), P()),
        out_specs=(P("tm", "col", None), P("tm", "col", None)),
        check_vma=False,
    )
```

```python
import functools

import jax
import jax.numpy as jnp
from jax import lax
from jax.experimental import pallas as pl
from jax.experimental.pallas import tpu as pltpu
from jax.sharding import PartitionSpec as P

GRID = 16
SLOTS = 3
META = 8
BF, F32 = jnp.bfloat16, jnp.float32
VMEM_BYTES = 44 * 2**20
QUADS_BYTES = 2**24
PACK_VMEM_BYTES = 60 * 2**20


def lanes(steps):
    at, places = 0, []
    for size in (steps, steps, steps, steps // 2, steps // 4, steps // 4, steps // 8, steps // 8, 1):
        places.append(at)
        at += size
    return places


def halves(value):
    high = value.astype(BF)
    return high, (value - high.astype(F32)).astype(BF)


def dot(a, b):
    return jnp.dot(a, b, preferred_element_type=F32)


def rows_product(rows, high, low):
    m = rows.shape[0]
    rows_high, rows_low = halves(rows)
    both = dot(jnp.concatenate([rows_high, rows_low], 0), high)
    return both[:m] + both[m:] + dot(rows_high, low)


def from_cell(value, shift):
    cells = value.shape[-1]
    return pltpu.roll(value, (-shift) % cells, 1) if shift % cells else value


SHIFTS = (0, 1, -1, GRID, -GRID)


def stencils(diffusivity):
    cell = lax.broadcasted_iota(jnp.int32, diffusivity.shape, 1)
    cells = diffusivity.shape[1]
    row, column = cell // GRID, cell % GRID
    inside = {1: column < GRID - 1, -1: column > 0, GRID: row < cells // GRID - 1, -GRID: row > 0}
    parts = {
        s: jnp.where(inside[s], 0.5 * (diffusivity + from_cell(diffusivity, s)), 0.0)
        for s in SHIFTS[1:]
    }
    parts[0] = 1.0 - (parts[1] + parts[-1] + parts[GRID] + parts[-GRID])
    return parts


def two_step_shifts():
    return sorted({a + b for a in SHIFTS for b in SHIFTS}, key=abs)


def tree_sum(terms):
    while len(terms) > 1:
        terms = [sum(terms[i + 1 : i + 2], terms[i]) for i in range(0, len(terms), 2)]
    return terms[0]


def apply_stencil(weights, shifts, value):
    return tree_sum([weights[k : k + 1] * from_cell(value, s) for k, s in enumerate(shifts)])


def folded_lane(cells, lane):
    half, rest = lane // (cells // 2), lax.rem(lane, cells // 2)
    return rest // (GRID // 2) * GRID + lax.rem(rest, GRID // 2) * 2 + half


def apply_folded(weights, shifts, value):
    half = value.shape[1] // 2
    parts, rolled = (value[:, :half], value[:, half:]), {}

    def moved(part, by):
        if (part, by) not in rolled:
            rolled[part, by] = from_cell(parts[part], by)
        return rolled[part, by]

    out = []
    for h in (0, 1):
        terms = []
        for k, s in enumerate(shifts):
            down = (s + GRID // 2) // GRID
            across = h + s - down * GRID
            terms.append(weights[k : k + 1, h * half : (h + 1) * half] * moved(across % 2, down * (GRID // 2) + across // 2))
        out.append(tree_sum(terms))
    return jnp.concatenate(out, 1)


def reorder(rows, order):
    m = rows.shape[0]
    high = rows.astype(BF)
    rest = rows - high.astype(F32)
    middle = rest.astype(BF)
    low = (rest - middle.astype(F32)).astype(BF)
    parts = dot(jnp.concatenate([high, middle, low], 0), order)
    return parts[:m] + (parts[m : 2 * m] + parts[2 * m :])


def folded_rows(value, space):
    cells = value.shape[0]
    starts = [r * GRID + h for h in (0, 1) for r in range(cells // GRID)]
    columns = []
    for i in range(space.shape[0]):
        space[i] = value[:, i * 128 : (i + 1) * 128]
        columns.append(jnp.concatenate([space[i, pl.ds(at, GRID // 2, stride=2), :] for at in starts], 0))
    return jnp.concatenate(columns, 1)


def tables_kernel(
    bands, diffusivity, gain, back, start, one, two, gain_high, gain_low, next_high, next_low, back_high, back_low, fold, unfold,
    first_rows, space, natural,
):
    cells = diffusivity.shape[1]
    index = [lax.broadcasted_iota(jnp.int32, (cells, cells), d) for d in (0, 1)]
    fold[...] = (index[0] == folded_lane(cells, index[1])).astype(F32).astype(BF)
    unfold[...] = (index[1] == folded_lane(cells, index[0])).astype(F32).astype(BF)
    unit = (index[0] == index[1]).astype(F32)
    first = stencils(diffusivity[...])
    natural[...] = jnp.zeros(natural.shape, F32)
    for b in range(bands):
        for k, s in enumerate(SHIFTS):
            natural[b * 8 + k : b * 8 + k + 1, :] = first[s][b : b + 1]
    own_rows = bands * 8
    for b in range(bands):
        for c in range(bands):
            total = {}
            for s in SHIFTS:
                for r in SHIFTS:
                    term = first[s][c : c + 1] * from_cell(first[r][b : b + 1], s)
                    total[s + r] = total[s + r] + term if s + r in total else term
            for k, s in enumerate(two_step_shifts()):
                at = own_rows + (b * bands + c) * 16 + k
                natural[at : at + 1, :] = total[s]
    at = own_rows + bands * bands * 16
    natural[at : at + 1, :] = start[...]
    folded = reorder(natural[...], fold[...])
    one[...] = folded[:own_rows].reshape(one.shape)
    two[...] = folded[own_rows:at].reshape(two.shape)
    first_rows[...] = jnp.broadcast_to(folded[at : at + 1], first_rows.shape)
    for b in range(bands):
        weights = natural[b * 8 : b * 8 + 8, :]
        gain_high[b], gain_low[b] = halves(folded_rows(gain[b], space.at[b, 0]).T)
        after = apply_stencil(weights, SHIFTS, unit - gain[b])
        after = folded_rows(after, space.at[b, 1]).T
        next_high[b], next_low[b] = halves(folded_rows(after, space.at[b, 2]))
        after = folded_rows(back[b], space.at[b, 3]).T
        back_high[b], back_low[b] = halves(folded_rows(after, space.at[b, 4]))


def pairs_kernel(bands, back_high, back_low, pair_high, pair_low):
    def pair(i, carry):
        earlier, later = i // bands, i % bands
        high, low = back_high[later], back_low[later]
        product = dot(high, back_high[earlier]) + (dot(low, back_high[earlier]) + dot(high, back_low[earlier]))
        pair_high[i], pair_low[i] = halves(product)
        return carry

    lax.fori_loop(0, bands * bands, pair, 0, unroll=4)


def pack_kernel(
    bands, band_far, mask_far, observations_far, diffusivity_far, gain, back, message, band, mask, observations, diffusivity, one,
    gain_here, back_here, delta, sem,
):
    steps, records, states = observations.shape
    near = (band, mask, observations, diffusivity)
    copies = [
        pltpu.make_async_copy(a, b, sem.at[i])
        for i, (a, b) in enumerate(zip((band_far, mask_far, observations_far, diffusivity_far), near))
    ]
    for copy in copies:
        copy.start()
    for copy in copies[:2]:
        copy.wait()
    lane = lax.broadcasted_iota(jnp.int32, (META, states), 1)
    meta = jnp.zeros((META, states), jnp.int32)
    band_at, mask_at, slot_at, pair_at, quad_at, quad_own_at, oct_at, oct_own_at, count_at = lanes(steps)

    def put(at, value):
        return jnp.where(lane == at, value, meta)

    count = jnp.int32(0)
    for t in range(steps):
        meta = put(band_at + t, band[t])
        meta = put(mask_at + t, mask[t])
        meta = put(slot_at + t, count)
        count = count + mask[t]
    packed = count > SLOTS
    for p in range(steps // 2):
        meta = put(pair_at + p, band[2 * p] * bands + band[2 * p + 1])
    ways, ways_own = [], []
    for q in range(steps // 4):
        m = [mask[4 * q + k] for k in range(4)]
        seen = m[0] + m[1] + m[2] + m[3]
        way = jnp.where(seen == 1, 2 + m[1] + 2 * m[2] + 3 * m[3], jnp.where(seen > 1, 1, 0))
        ways_own.append(way)
        ways.append(jnp.where(packed & ((seen > 0) | (q in (0, steps // 4 - 1))), 1, way))
        meta = put(quad_at + q, ways[q])
        meta = put(quad_own_at + q, way)
    for o in range(steps // 8):
        meta = put(oct_at + o, ways[2 * o] + ways[2 * o + 1])
        meta = put(oct_own_at + o, ways_own[2 * o] + ways_own[2 * o + 1])
    meta = put(count_at, count)
    message[SLOTS * records :, :] = meta.astype(F32)
    for copy in copies[2:]:
        copy.wait()
    at = jnp.int32(0)
    for t in range(steps):

        @pl.when((mask[t] > 0) & (at < SLOTS))
        def _(t=t, at=at):
            message[pl.ds(pl.multiple_of(at * records, 8), records), :] = observations[t]

        at = at + mask[t]

    for slot in range(SLOTS):

        @pl.when(count <= slot)
        def _(slot=slot):
            message[slot * records : (slot + 1) * records, :] = jnp.zeros((records, states), F32)

    @pl.when(packed)
    def _():
        copies = [pltpu.make_async_copy(a, b, sem.at[i]) for i, (a, b) in enumerate(((gain, gain_here), (back, back_here)))]
        for copy in copies:
            copy.start()
        first = stencils(diffusivity[...])
        for b in range(bands):
            for k, s in enumerate(SHIFTS):
                one[b, k : k + 1, :] = first[s][b : b + 1]
        for copy in copies:
            copy.wait()

        def times(rows, matrix):
            return lax.dot_general(
                rows, matrix, (((1,), (1,)), ((), ())), precision=lax.Precision.HIGHEST, preferred_element_type=F32
            )

        def forward(t, x):
            p = apply_stencil(one[band[t]], SHIFTS, x)
            delta[t] = mask[t].astype(F32) * times(observations[t] - p, gain_here[band[t]])
            return p + delta[t]

        zeros = jnp.zeros((records, states), F32)
        message[0:records, :] = lax.fori_loop(0, steps, forward, zeros)

        def backward(i, r):
            t = steps - 1 - i
            return times(r, back_here[band[t]]) + delta[t]

        message[records : 2 * records, :] = lax.fori_loop(0, steps, backward, zeros)


def main_kernel(*args):
    records, states = args[4].shape[1:]
    small = [[pltpu.ACC(i)((records, states), F32) for i in (0, 1)] for _ in range(4)]
    large = [pltpu.ACC(i)((states // 2, states), F32) for i in (0, 1)]
    pl.run_scoped(functools.partial(filter_and_smooth, *args), small, large, pltpu.ACC(0)((4 * records, states), F32))


def times_many(products, sums):
    for i, (rows, high, low) in enumerate(products):
        rows_high, rows_low = halves(rows)
        pltpu.matmul_push_rhs(high, i % 2, 0)
        pltpu.matmul_push_rhs(low, i % 2, 1)
        pltpu.matmul_acc_lhs(sums[i][0], rows_high, load_staged_rhs=i % 2)
        pltpu.matmul_acc_lhs(sums[i][1], rows_high, load_staged_rhs=i % 2)
        pltpu.matmul_acc_lhs(sums[i][0], rows_low)
    return [pltpu.matmul_pop(a) + pltpu.matmul_pop(b) for a, b in sums[: len(products)]]


def filter_and_smooth(
    bands,
    devices,
    fields,
    pieces,
    observations,
    *refs,
):
    refs, (small, large, many) = refs[:-3], refs[-3:]

    def rows_product(rows, high, low):
        return times_many([(rows, high, low)], small)[0]

    def reorder(rows, order, sums=None):
        sums = sums or [many if rows.shape[0] == many.shape[0] else small[0][0]]
        each = rows.shape[0] // len(sums)
        for i, into in enumerate(sums):
            pltpu.matmul_push_rhs(order, 0, i)
            part = rows[i * each : (i + 1) * each]
            high = part.astype(BF)
            rest = part - high.astype(F32)
            middle = rest.astype(BF)
            pltpu.matmul_acc_lhs(into, (rest - middle.astype(F32)).astype(BF), load_staged_rhs=0)
            pltpu.matmul_acc_lhs(into, middle)
            pltpu.matmul_acc_lhs(into, high)
        return jnp.concatenate([pltpu.matmul_pop(into) for into in sums], 0)

    parts, refs = refs[:pieces], refs[pieces:]
    (one, two, gain_high, gain_low, next_high, next_low, back_high, back_low, fold, unfold, first_rows), refs = refs[:11], refs[11:]
    (pair_high, pair_low, filtered_far, smoothed_far, held, outward, ready, after, ends, out_sem), refs = refs[:10], refs[10:]
    (inbox, meta, table, delta, pushed, sem), quads = refs[:6], refs[6:]
    steps, records, states = observations.shape
    per = steps // 4
    rows = parts[0].shape[0] // (devices // pieces)
    me = lax.axis_index("tm")

    def place(apart):
        found, scale = jnp.int32(0), 1
        for shift, width in reversed(fields):
            found = found + lax.bitwise_and(lax.shift_right_logical(apart, shift), width - 1) * scale
            scale *= width
        return found

    def apart_at(position):
        apart, position = 0, int(position)
        for shift, width in reversed(fields):
            apart |= (position % width) << shift
            position //= width
        return apart

    each = parts[0].shape[0]
    for k in range(devices):
        at = k * rows + SLOTS * records - k * rows // each * each
        block = lax.bitwise_xor(me, apart_at(k))
        meta[pl.ds(block, 1), :] = parts[k * rows // each][at : at + 1, :].astype(jnp.int32)
    copy = pltpu.make_async_copy(meta, table, sem)
    copy.start()
    for i, part in enumerate(parts):
        inbox[i * each : (i + 1) * each, :] = part[...]
    copy.wait()

    def step(b, x):
        return apply_folded(one[b], SHIFTS, x)

    def two_steps(pair, x):
        return apply_folded(two[pair], two_step_shifts(), x)

    def observed_step(b, x, y):
        return sum(times_many([(y, gain_high[b], gain_low[b]), (x, next_high[b], next_low[b])], small))

    def back(b, r):
        return rows_product(r, back_high[b], back_low[b])

    def back_two(pair, r):
        return rows_product(r, pair_high[pair], pair_low[pair])

    band_at, mask_at, slot_at, pair_at, quad_at, quad_own_at, oct_at, oct_own_at, count_at = lanes(steps)

    def pairs(block, q):
        return table[block, pair_at + 2 * q], table[block, pair_at + 2 * q + 1]

    def four(at, block, q):
        return [table[block, at + 4 * q + k] for k in range(4)]

    def prepare(block, q):
        if not quads:
            return lambda: None
        right, left = pairs(block, q)
        high, low = pair_high[left], pair_low[left]
        n = states // 2
        for i in (0, 1):
            pltpu.matmul_push_rhs(pair_high[right], 0, i)
            pltpu.matmul_push_rhs(pair_low[right], 1, i)
            into = large[i]
            h, l = high[i * n : (i + 1) * n], low[i * n : (i + 1) * n]
            pltpu.matmul_acc_lhs(into, h, load_staged_rhs=0)
            pltpu.matmul_acc_lhs(into, l)
            pltpu.matmul_acc_lhs(into, h, load_staged_rhs=1)

        def finish():
            for i in (0, 1):
                rows = pl.ds(i * n, n)
                quads[0][block * per + q, rows, :], quads[1][block * per + q, rows, :] = halves(pltpu.matmul_pop(large[i]))

        return finish

    def over_quad(block, q, r):
        if quads:
            return rows_product(r, quads[0][block * per + q], quads[1][block * per + q])
        early, late = pairs(block, q)
        return back_two(early, back_two(late, r))

    def added(seen, at, r):
        return jnp.where(seen > 0, r + delta[at], r)

    def plain(block, q, x):
        early, late = pairs(block, q)
        at = (block * per + q) * 4 + 1
        finish = prepare(block, q)
        pushed[block * per + q] = jnp.zeros_like(x)
        x = two_steps(early, x)
        held[at + 1] = x
        finish()
        x = two_steps(late, x)
        held[at + 3] = x
        return x

    def filter_quad(block, q, x):
        at = (block * per + q) * 4
        own = block == me
        first = pl.multiple_of(place(lax.bitwise_xor(block, me)) * rows, 8)

        def keep(k, x):
            held[at + k + 1] = x
            return x

        def corrected(b, k, x, packed=False):
            slot = lax.rem(table[block, slot_at + 4 * q + k], SLOTS)
            sent = inbox[pl.ds(pl.multiple_of(first + slot * records, 8), records), :]
            y = jnp.where(packed, 0.0, jnp.where(own, observations[4 * q + k], sent))
            p, x = step(b, x), observed_step(b, x, y)
            delta[at + k] = x - p
            held[at + k + 1] = x
            return x

        def one_seen(k, x):
            b = four(band_at, block, q)
            early, late = pairs(block, q)
            finish = prepare(block, q)
            if k >= 2:
                x = keep(1, two_steps(early, x))
            if k % 2:
                x = keep(k - 1, step(b[k - 1], x))
            x = corrected(b[k], k, x)
            change = delta[at + k]
            if k % 2 == 0:
                x = keep(k + 1, step(b[k + 1], x))
            if k < 2:
                x = keep(3, two_steps(late, x))
            if k == 0:
                change = jnp.zeros_like(x)
            elif k == 1:
                change = back(b[0], change)
            else:
                change = back_two(early, change if k == 2 else back(b[2], change))
            pushed[block * per + q] = change
            finish()
            return x

        def any_seen(x):
            b, m = four(band_at, block, q), four(mask_at, block, q)
            packed = (table[block, count_at] > SLOTS) & jnp.logical_not(own)
            prepare(block, q)()
            for k in range(4):
                x = lax.cond(
                    m[k] > 0,
                    lambda x, k=k: corrected(b[k], k, x, packed),
                    lambda x, k=k: keep(k, step(b[k], x)),
                    x,
                )
            r = jnp.zeros_like(x)
            for k in (3, 2, 1):
                r = back(b[k - 1], added(m[k], at + k, r))
            pushed[block * per + q] = r

            def add_sent(slot):
                sent = inbox[pl.ds(pl.multiple_of(first + slot * records, 8), records), :]
                return lambda x: x + reorder(sent, fold[...])

            pushed[block * per + q] = lax.cond(packed & (q == 0), add_sent(1), lambda r: r, r)
            return keep(3, lax.cond(packed & (q == per - 1), add_sent(0), lambda x: x, x))

        return lax.switch(
            table[block, jnp.where(own, quad_own_at, quad_at) + q],
            [functools.partial(plain, block, q), any_seen] + [functools.partial(one_seen, k) for k in range(4)],
            x,
        )

    def filter_oct(block, o, x):
        return lax.cond(
            table[block, jnp.where(block == me, oct_own_at, oct_at) + o] == 0,
            lambda x: plain(block, 2 * o + 1, plain(block, 2 * o, x)),
            lambda x: lax.fori_loop(2 * o, 2 * o + 2, functools.partial(filter_quad, block), x),
            x,
        )

    def filter_block(block, x):
        return lax.fori_loop(0, per // 2, functools.partial(filter_oct, block), x)

    held[0] = first_rows[...]
    x = lax.fori_loop(0, me + 1, filter_block, held[0])
    own_bands = [four(band_at, me, q) for q in range(per)]
    own_masks = [four(mask_at, me, q) for q in range(per)]
    for q in range(per):
        for k in (0, 2):
            at = me * steps + q * 4 + k
            seen = own_masks[q][k] + own_masks[q][k + 1] > 0
            held[at + 1] = jnp.where(seen, held[at + 1], step(own_bands[q][k], held[at]))
    outs = [pltpu.make_async_copy(outward.at[k], smoothed_far.at[:, k], out_sem.at[k]) for k in range(4)]
    outs.append(pltpu.make_async_copy(ready, filtered_far, out_sem.at[4]))
    lax.fori_loop(me + 1, devices, filter_block, x)

    def smooth_quad(block, q, r, gains):
        after[q] = r
        e = gains(block, q, r) + pushed[block * per + q]
        ends[q] = e
        return added(table[block, mask_at + 4 * q], block * steps + 4 * q, e)

    def smooth_all(gains):
        def smooth_block(i, r):
            for q in reversed(range(per)):
                r = smooth_quad(devices - 1 - i, q, r, gains)
            return r

        lax.fori_loop(0, devices - me, smooth_block, jnp.zeros((records, states), F32))

    def smooth_staged():
        high_sum, low_sum = small[0]

        def stage(quad):
            pltpu.matmul_push_rhs(quads[0][quad], 0, 0)
            pltpu.matmul_push_rhs(quads[1][quad], 0, 1)

        def multiply(high, low):
            pltpu.matmul_acc_lhs(high_sum, high, load_staged_rhs=0)
            pltpu.matmul_acc_lhs(low_sum, high, load_staged_rhs=0)
            pltpu.matmul_acc_lhs(high_sum, low)

        def gains(block, q, r):
            multiply(*halves(r))
            stage(jnp.maximum(block * per + q - 1, 0))
            return pltpu.matmul_pop(high_sum) + pltpu.matmul_pop(low_sum)

        stage(devices * per - 1)
        smooth_all(gains)
        none = jnp.zeros((records, states), BF)
        multiply(none, none)
        ends[per] = pltpu.matmul_pop(high_sum) + pltpu.matmul_pop(low_sum)

    if quads:
        smooth_staged()
    else:
        smooth_all(over_quad)

    own_held = held[pl.ds(me * steps + 1, steps)].reshape(steps * records, states)
    ready[...] = reorder(own_held, unfold[...], large).reshape(ready.shape)
    outs[4].start()

    def leave(k, after):
        rows_out = jnp.concatenate([held[me * steps + q * 4 + k + 1] + after[q] for q in range(per)], 0)
        outward[k] = reorder(rows_out, unfold[...]).reshape(outward.shape[1:])
        outs[k].start()
        return [added(own_masks[q][k], me * steps + q * 4 + k, after[q]) for q in range(per)]

    leave(0, [ends[q] for q in range(per)])
    r = [after[q] for q in range(per)]
    for k in (3, 2, 1):
        b = [own_bands[q][k] for q in range(per)]
        r = leave(k, times_many([(r[q], back_high[b[q]], back_low[b[q]]) for q in range(per)], small))
    for copy in outs:
        copy.wait()


def whole(memory=pltpu.VMEM):
    return pl.BlockSpec(memory_space=memory)


def xor_round(held, low, width, devices):
    return [held] + [
        lax.ppermute(held, "tm", [(i, i ^ (k << low)) for i in range(devices)]) for k in range(1, 1 << width)
    ]


def shards(observations, band_index, obs_mask, diffusivity, gain, back, initial_mean):
    steps, records, states = observations.shape
    bands = diffusivity.shape[0]
    devices = lax.axis_size("tm")
    rows = SLOTS * records + META
    params = pltpu.CompilerParams(vmem_limit_bytes=VMEM_BYTES)
    shape = jax.ShapeDtypeStruct
    message = pl.pallas_call(
        functools.partial(pack_kernel, bands),
        out_shape=shape((rows, states), F32),
        in_specs=[whole(pltpu.HBM)] * 6,
        out_specs=whole(),
        scratch_shapes=[
            pltpu.SMEM((steps,), jnp.int32),
            pltpu.SMEM((steps,), jnp.int32),
            pltpu.VMEM((steps, records, states), F32),
            pltpu.VMEM((bands, states), F32),
            pltpu.VMEM((bands, 8, states), F32),
            pltpu.VMEM((bands, states, states), F32),
            pltpu.VMEM((bands, states, states), F32),
            pltpu.VMEM((steps, records, states), F32),
            pltpu.SemaphoreType.DMA((4,)),
        ],
        compiler_params=pltpu.CompilerParams(vmem_limit_bytes=PACK_VMEM_BYTES),
        name="pack_message",
    )(band_index, obs_mask, observations, diffusivity, gain, back)
    matrix = lambda count: shape((count, states, states), BF)
    cost = lambda flops: pl.CostEstimate(flops=flops, bytes_accessed=4 * 2**20, transcendentals=0)

    def make_tables():
        return pl.pallas_call(
            functools.partial(tables_kernel, bands),
            out_shape=[shape((bands, 8, states), F32), shape((bands * bands, 16, states), F32)]
            + [matrix(bands)] * 6
            + [shape((states, states), BF)] * 2
            + [shape((records, states), F32)],
            in_specs=[whole()] * 4,
            out_specs=[whole()] * 11,
            scratch_shapes=[
                pltpu.VMEM((bands, 5, states // 128, states, 128), F32),
                pltpu.VMEM((bands * 8 + bands * bands * 16 + 8, states), F32),
            ],
            compiler_params=params,
            cost_estimate=cost(2**28),
            name="tables",
        )(diffusivity, gain, back, initial_mean[None, :])

    def make_pairs(back_high, back_low):
        return pl.pallas_call(
            functools.partial(pairs_kernel, bands),
            out_shape=[matrix(bands * bands)] * 2,
            in_specs=[whole()] * 2,
            out_specs=[whole()] * 2,
            compiler_params=params,
            cost_estimate=cost(6 * bands**2 * states**3),
            name="pairs",
        )(back_high, back_low)

    bits = devices.bit_length() - 1
    pieces, fields, low, tables = [message], [], bits, None
    for width in [1] * (bits % 2) + [2] * (bits // 2):
        low -= width
        held = jnp.concatenate(pieces, 0)
        if fields and tables is None:
            tables = make_tables()
            held, tables = lax.optimization_barrier((held, tables))
        pieces = xor_round(held, low, width, devices)
        fields = [(low, 1 << width)] + fields
    tables = make_tables() if tables is None else tables
    tables = [*tables, *make_pairs(*tables[6:8])]
    out = shape((steps // 4, 4, records, states), F32)
    quads = devices * steps // 4
    deep = quads * states * states * 4 <= QUADS_BYTES
    filtered, smoothed = pl.pallas_call(
        functools.partial(main_kernel, bands, devices, fields, len(pieces)),
        out_shape=[out, out],
        in_specs=[whole()] * (1 + len(pieces) + len(tables)),
        out_specs=[whole(pltpu.HBM)] * 2,
        scratch_shapes=[
            pltpu.VMEM((devices * steps + 1, records, states), F32),
            pltpu.VMEM((4, steps // 4, records, states), F32),
            pltpu.VMEM((steps // 4, 4, records, states), F32),
            pltpu.VMEM((steps // 4, records, states), F32),
            pltpu.VMEM((steps // 4 + 1, records, states), F32),
            pltpu.SemaphoreType.DMA((5,)),
            pltpu.VMEM((devices * rows, states), F32),
            pltpu.VMEM((devices, states), jnp.int32),
            pltpu.SMEM((devices, states), jnp.int32),
            pltpu.VMEM((devices * steps, records, states), F32),
            pltpu.VMEM((quads, records, states), F32),
            pltpu.SemaphoreType.DMA,
        ]
        + [pltpu.VMEM((quads, states, states), BF)] * (2 * deep),
        compiler_params=params,
        name="filter_and_smooth",
    )(observations, *pieces, *tables)
    return filtered.reshape(observations.shape), smoothed.reshape(observations.shape)


def solution(mesh):
    return jax.shard_map(
        shards,
        mesh=mesh,
        in_specs=(P("tm", "col", None), P("tm"), P("tm"), P(), P(), P(), P()),
        out_specs=(P("tm", "col", None), P("tm", "col", None)),
        check_vma=False,
    )
```

```python
import functools

import jax
import jax.numpy as jnp
from jax import lax
from jax.experimental import pallas as pl
from jax.experimental.pallas import tpu as pltpu
from jax.sharding import PartitionSpec as P

GRID = 16
SLOTS = 3
META = 8
BF, F32 = jnp.bfloat16, jnp.float32
VMEM_BYTES = 44 * 2**20
QUADS_BYTES = 2**24
PACK_VMEM_BYTES = 60 * 2**20


def lanes(steps):
    at, places = 0, []
    for size in (steps, steps, steps, steps // 2, steps // 4, steps // 4, steps // 8, steps // 8, 1):
        places.append(at)
        at += size
    return places


def halves(value):
    high = value.astype(BF)
    return high, (value - high.astype(F32)).astype(BF)


def dot(a, b):
    return jnp.dot(a, b, preferred_element_type=F32)


def rows_product(rows, high, low):
    m = rows.shape[0]
    rows_high, rows_low = halves(rows)
    both = dot(jnp.concatenate([rows_high, rows_low], 0), high)
    return both[:m] + both[m:] + dot(rows_high, low)


def from_cell(value, shift):
    cells = value.shape[-1]
    return pltpu.roll(value, (-shift) % cells, 1) if shift % cells else value


SHIFTS = (0, 1, -1, GRID, -GRID)


def stencils(diffusivity):
    cell = lax.broadcasted_iota(jnp.int32, diffusivity.shape, 1)
    cells = diffusivity.shape[1]
    row, column = cell // GRID, cell % GRID
    inside = {1: column < GRID - 1, -1: column > 0, GRID: row < cells // GRID - 1, -GRID: row > 0}
    parts = {
        s: jnp.where(inside[s], 0.5 * (diffusivity + from_cell(diffusivity, s)), 0.0)
        for s in SHIFTS[1:]
    }
    parts[0] = 1.0 - (parts[1] + parts[-1] + parts[GRID] + parts[-GRID])
    return parts


def two_step_shifts():
    return sorted({a + b for a in SHIFTS for b in SHIFTS}, key=abs)


def tree_sum(terms):
    while len(terms) > 1:
        terms = [sum(terms[i + 1 : i + 2], terms[i]) for i in range(0, len(terms), 2)]
    return terms[0]


def apply_stencil(weights, shifts, value):
    return tree_sum([weights[k : k + 1] * from_cell(value, s) for k, s in enumerate(shifts)])


def folded_lane(cells, lane):
    half, rest = lane // (cells // 2), lax.rem(lane, cells // 2)
    return rest // (GRID // 2) * GRID + lax.rem(rest, GRID // 2) * 2 + half


def apply_folded(weights, shifts, value):
    half = value.shape[1] // 2
    parts, rolled = (value[:, :half], value[:, half:]), {}

    def moved(part, by):
        if (part, by) not in rolled:
            rolled[part, by] = from_cell(parts[part], by)
        return rolled[part, by]

    out = []
    for h in (0, 1):
        terms = []
        for k, s in enumerate(shifts):
            down = (s + GRID // 2) // GRID
            across = h + s - down * GRID
            terms.append(weights[k : k + 1, h * half : (h + 1) * half] * moved(across % 2, down * (GRID // 2) + across // 2))
        out.append(tree_sum(terms))
    return jnp.concatenate(out, 1)


def reorder(rows, order):
    m = rows.shape[0]
    high = rows.astype(BF)
    rest = rows - high.astype(F32)
    middle = rest.astype(BF)
    low = (rest - middle.astype(F32)).astype(BF)
    parts = dot(jnp.concatenate([high, middle, low], 0), order)
    return parts[:m] + (parts[m : 2 * m] + parts[2 * m :])


def folded_rows(value, space):
    cells = value.shape[0]
    starts = [r * GRID + h for h in (0, 1) for r in range(cells // GRID)]
    columns = []
    for i in range(space.shape[0]):
        space[i] = value[:, i * 128 : (i + 1) * 128]
        columns.append(jnp.concatenate([space[i, pl.ds(at, GRID // 2, stride=2), :] for at in starts], 0))
    return jnp.concatenate(columns, 1)


def tables_kernel(
    bands, diffusivity, gain, back, start, one, two, gain_high, gain_low, next_high, next_low, back_high, back_low, fold, unfold,
    first_rows, space, natural,
):
    cells = diffusivity.shape[1]
    index = [lax.broadcasted_iota(jnp.int32, (cells, cells), d) for d in (0, 1)]
    fold[...] = (index[0] == folded_lane(cells, index[1])).astype(F32).astype(BF)
    unfold[...] = (index[1] == folded_lane(cells, index[0])).astype(F32).astype(BF)
    unit = (index[0] == index[1]).astype(F32)
    first = stencils(diffusivity[...])
    natural[...] = jnp.zeros(natural.shape, F32)
    for b in range(bands):
        for k, s in enumerate(SHIFTS):
            natural[b * 8 + k : b * 8 + k + 1, :] = first[s][b : b + 1]
    own_rows = bands * 8
    for b in range(bands):
        for c in range(bands):
            total = {}
            for s in SHIFTS:
                for r in SHIFTS:
                    term = first[s][c : c + 1] * from_cell(first[r][b : b + 1], s)
                    total[s + r] = total[s + r] + term if s + r in total else term
            for k, s in enumerate(two_step_shifts()):
                at = own_rows + (b * bands + c) * 16 + k
                natural[at : at + 1, :] = total[s]
    at = own_rows + bands * bands * 16
    natural[at : at + 1, :] = start[...]
    folded = reorder(natural[...], fold[...])
    one[...] = folded[:own_rows].reshape(one.shape)
    two[...] = folded[own_rows:at].reshape(two.shape)
    first_rows[...] = jnp.broadcast_to(folded[at : at + 1], first_rows.shape)
    for b in range(bands):
        weights = natural[b * 8 : b * 8 + 8, :]
        gain_high[b], gain_low[b] = halves(folded_rows(gain[b], space.at[b, 0]).T)
        after = apply_stencil(weights, SHIFTS, unit - gain[b])
        after = folded_rows(after, space.at[b, 1]).T
        next_high[b], next_low[b] = halves(folded_rows(after, space.at[b, 2]))
        after = folded_rows(back[b], space.at[b, 3]).T
        back_high[b], back_low[b] = halves(folded_rows(after, space.at[b, 4]))


def pairs_kernel(bands, back_high, back_low, pair_high, pair_low):
    def pair(i, carry):
        earlier, later = i // bands, i % bands
        high, low = back_high[later], back_low[later]
        product = dot(high, back_high[earlier]) + (dot(low, back_high[earlier]) + dot(high, back_low[earlier]))
        pair_high[i], pair_low[i] = halves(product)
        return carry

    lax.fori_loop(0, bands * bands, pair, 0, unroll=4)


def pack_kernel(
    bands, band_far, mask_far, observations_far, diffusivity_far, gain, back, message, band, mask, observations, diffusivity, one,
    gain_here, back_here, delta, sem,
):
    steps, records, states = observations.shape
    near = (band, mask, observations, diffusivity)
    copies = [
        pltpu.make_async_copy(a, b, sem.at[i])
        for i, (a, b) in enumerate(zip((band_far, mask_far, observations_far, diffusivity_far), near))
    ]
    for copy in copies:
        copy.start()
    for copy in copies[:2]:
        copy.wait()
    lane = lax.broadcasted_iota(jnp.int32, (META, states), 1)
    meta = jnp.zeros((META, states), jnp.int32)
    band_at, mask_at, slot_at, pair_at, quad_at, quad_own_at, oct_at, oct_own_at, count_at = lanes(steps)

    def put(at, value):
        return jnp.where(lane == at, value, meta)

    count = jnp.int32(0)
    for t in range(steps):
        meta = put(band_at + t, band[t])
        meta = put(mask_at + t, mask[t])
        meta = put(slot_at + t, count)
        count = count + mask[t]
    packed = count > SLOTS
    for p in range(steps // 2):
        meta = put(pair_at + p, band[2 * p] * bands + band[2 * p + 1])
    ways, ways_own = [], []
    for q in range(steps // 4):
        m = [mask[4 * q + k] for k in range(4)]
        seen = m[0] + m[1] + m[2] + m[3]
        way = jnp.where(seen == 1, 2 + m[1] + 2 * m[2] + 3 * m[3], jnp.where(seen > 1, 1, 0))
        ways_own.append(way)
        ways.append(jnp.where(packed & ((seen > 0) | (q in (0, steps // 4 - 1))), 1, way))
        meta = put(quad_at + q, ways[q])
        meta = put(quad_own_at + q, way)
    for o in range(steps // 8):
        meta = put(oct_at + o, ways[2 * o] + ways[2 * o + 1])
        meta = put(oct_own_at + o, ways_own[2 * o] + ways_own[2 * o + 1])
    meta = put(count_at, count)
    message[SLOTS * records :, :] = meta.astype(F32)
    for copy in copies[2:]:
        copy.wait()
    at = jnp.int32(0)
    for t in range(steps):

        @pl.when((mask[t] > 0) & (at < SLOTS))
        def _(t=t, at=at):
            message[pl.ds(pl.multiple_of(at * records, 8), records), :] = observations[t]

        at = at + mask[t]

    for slot in range(SLOTS):

        @pl.when(count <= slot)
        def _(slot=slot):
            message[slot * records : (slot + 1) * records, :] = jnp.zeros((records, states), F32)

    @pl.when(packed)
    def _():
        copies = [pltpu.make_async_copy(a, b, sem.at[i]) for i, (a, b) in enumerate(((gain, gain_here), (back, back_here)))]
        for copy in copies:
            copy.start()
        first = stencils(diffusivity[...])
        for b in range(bands):
            for k, s in enumerate(SHIFTS):
                one[b, k : k + 1, :] = first[s][b : b + 1]
        for copy in copies:
            copy.wait()

        def times(rows, matrix):
            return lax.dot_general(
                rows, matrix, (((1,), (1,)), ((), ())), precision=lax.Precision.HIGHEST, preferred_element_type=F32
            )

        def forward(t, x):
            p = apply_stencil(one[band[t]], SHIFTS, x)
            delta[t] = mask[t].astype(F32) * times(observations[t] - p, gain_here[band[t]])
            return p + delta[t]

        zeros = jnp.zeros((records, states), F32)
        message[0:records, :] = lax.fori_loop(0, steps, forward, zeros)

        def backward(i, r):
            t = steps - 1 - i
            return times(r, back_here[band[t]]) + delta[t]

        message[records : 2 * records, :] = lax.fori_loop(0, steps, backward, zeros)


def main_kernel(*args):
    records, states = args[4].shape[1:]
    small = [[pltpu.ACC(i)((records, states), F32) for i in (0, 1)] for _ in range(4)]
    large = [pltpu.ACC(i)((states // 2, states), F32) for i in (0, 1)]
    pl.run_scoped(functools.partial(filter_and_smooth, *args), small, large, pltpu.ACC(0)((4 * records, states), F32))


def times_many(products, sums, then=None):
    for i, (rows, high, low) in enumerate(products):
        rows_high, rows_low = halves(rows)
        pltpu.matmul_push_rhs(high, i % 2, 0)
        pltpu.matmul_push_rhs(low, i % 2, 1)
        pltpu.matmul_acc_lhs(sums[i][0], rows_high, load_staged_rhs=i % 2)
        pltpu.matmul_acc_lhs(sums[i][1], rows_high, load_staged_rhs=i % 2)
        pltpu.matmul_acc_lhs(sums[i][0], rows_low)
    if then is not None:
        pltpu.matmul_push_rhs(then, 0, 0)
    return [pltpu.matmul_pop(a) + pltpu.matmul_pop(b) for a, b in sums[: len(products)]]


def filter_and_smooth(
    bands,
    devices,
    fields,
    pieces,
    observations,
    *refs,
):
    refs, (small, large, many) = refs[:-3], refs[-3:]

    def rows_product(rows, high, low):
        return times_many([(rows, high, low)], small)[0]

    def reorder(rows, order, sums=None, staged=False):
        sums = sums or [many if rows.shape[0] == many.shape[0] else small[0][0]]
        each = rows.shape[0] // len(sums)
        for i, into in enumerate(sums):
            if not staged:
                pltpu.matmul_push_rhs(order, 0, i)
            part = rows[i * each : (i + 1) * each]
            high = part.astype(BF)
            rest = part - high.astype(F32)
            middle = rest.astype(BF)
            pltpu.matmul_acc_lhs(into, (rest - middle.astype(F32)).astype(BF), load_staged_rhs=0)
            pltpu.matmul_acc_lhs(into, middle)
            pltpu.matmul_acc_lhs(into, high)
        return jnp.concatenate([pltpu.matmul_pop(into) for into in sums], 0)

    parts, refs = refs[:pieces], refs[pieces:]
    (one, two, gain_high, gain_low, next_high, next_low, back_high, back_low, fold, unfold, first_rows), refs = refs[:11], refs[11:]
    (pair_high, pair_low, filtered_far, smoothed_far, held, outward, ready, after, ends, out_sem), refs = refs[:10], refs[10:]
    (inbox, meta, table, delta, pushed, sem), quads = refs[:6], refs[6:]
    steps, records, states = observations.shape
    per = steps // 4
    rows = parts[0].shape[0] // (devices // pieces)
    me = lax.axis_index("tm")

    def place(apart):
        found, scale = jnp.int32(0), 1
        for shift, width in reversed(fields):
            found = found + lax.bitwise_and(lax.shift_right_logical(apart, shift), width - 1) * scale
            scale *= width
        return found

    def apart_at(position):
        apart, position = 0, int(position)
        for shift, width in reversed(fields):
            apart |= (position % width) << shift
            position //= width
        return apart

    each = parts[0].shape[0]
    for k in range(devices):
        at = k * rows + SLOTS * records - k * rows // each * each
        block = lax.bitwise_xor(me, apart_at(k))
        meta[pl.ds(block, 1), :] = parts[k * rows // each][at : at + 1, :].astype(jnp.int32)
    copy = pltpu.make_async_copy(meta, table, sem)
    copy.start()
    for i, part in enumerate(parts):
        inbox[i * each : (i + 1) * each, :] = part[...]
    copy.wait()

    def step(b, x):
        return apply_folded(one[b], SHIFTS, x)

    def two_steps(pair, x):
        return apply_folded(two[pair], two_step_shifts(), x)

    def observed_step(b, x, y):
        return sum(times_many([(y, gain_high[b], gain_low[b]), (x, next_high[b], next_low[b])], small))

    def back(b, r):
        return rows_product(r, back_high[b], back_low[b])

    def back_two(pair, r):
        return rows_product(r, pair_high[pair], pair_low[pair])

    band_at, mask_at, slot_at, pair_at, quad_at, quad_own_at, oct_at, oct_own_at, count_at = lanes(steps)

    def pairs(block, q):
        return table[block, pair_at + 2 * q], table[block, pair_at + 2 * q + 1]

    def four(at, block, q):
        return [table[block, at + 4 * q + k] for k in range(4)]

    def prepare(block, q):
        if not quads:
            return lambda: None
        right, left = pairs(block, q)
        high, low = pair_high[left], pair_low[left]
        n = states // 2
        for i in (0, 1):
            pltpu.matmul_push_rhs(pair_high[right], 0, i)
            pltpu.matmul_push_rhs(pair_low[right], 1, i)
            into = large[i]
            h, l = high[i * n : (i + 1) * n], low[i * n : (i + 1) * n]
            pltpu.matmul_acc_lhs(into, h, load_staged_rhs=0)
            pltpu.matmul_acc_lhs(into, l)
            pltpu.matmul_acc_lhs(into, h, load_staged_rhs=1)

        def finish():
            for i in (0, 1):
                rows = pl.ds(i * n, n)
                quads[0][block * per + q, rows, :], quads[1][block * per + q, rows, :] = halves(pltpu.matmul_pop(large[i]))

        return finish

    def over_quad(block, q, r):
        if quads:
            return rows_product(r, quads[0][block * per + q], quads[1][block * per + q])
        early, late = pairs(block, q)
        return back_two(early, back_two(late, r))

    def added(seen, at, r):
        return jnp.where(seen > 0, r + delta[at], r)

    def plain(block, q, x):
        early, late = pairs(block, q)
        at = (block * per + q) * 4 + 1
        finish = prepare(block, q)
        pushed[block * per + q] = jnp.zeros_like(x)
        x = two_steps(early, x)
        held[at + 1] = x
        finish()
        x = two_steps(late, x)
        held[at + 3] = x
        return x

    def filter_quad(block, q, x):
        at = (block * per + q) * 4
        own = block == me
        first = pl.multiple_of(place(lax.bitwise_xor(block, me)) * rows, 8)

        def keep(k, x):
            held[at + k + 1] = x
            return x

        def corrected(b, k, x, packed=False):
            slot = lax.rem(table[block, slot_at + 4 * q + k], SLOTS)
            sent = inbox[pl.ds(pl.multiple_of(first + slot * records, 8), records), :]
            y = jnp.where(packed, 0.0, jnp.where(own, observations[4 * q + k], sent))
            p, x = step(b, x), observed_step(b, x, y)
            delta[at + k] = x - p
            held[at + k + 1] = x
            return x

        def one_seen(k, x):
            b = four(band_at, block, q)
            early, late = pairs(block, q)
            finish = prepare(block, q)
            if k >= 2:
                x = keep(1, two_steps(early, x))
            if k % 2:
                x = keep(k - 1, step(b[k - 1], x))
            x = corrected(b[k], k, x)
            change = delta[at + k]
            if k % 2 == 0:
                x = keep(k + 1, step(b[k + 1], x))
            if k < 2:
                x = keep(3, two_steps(late, x))
            if k == 0:
                change = jnp.zeros_like(x)
            elif k == 1:
                change = back(b[0], change)
            else:
                change = back_two(early, change if k == 2 else back(b[2], change))
            pushed[block * per + q] = change
            finish()
            return x

        def any_seen(x):
            b, m = four(band_at, block, q), four(mask_at, block, q)
            packed = (table[block, count_at] > SLOTS) & jnp.logical_not(own)
            prepare(block, q)()
            for k in range(4):
                x = lax.cond(
                    m[k] > 0,
                    lambda x, k=k: corrected(b[k], k, x, packed),
                    lambda x, k=k: keep(k, step(b[k], x)),
                    x,
                )
            r = jnp.zeros_like(x)
            for k in (3, 2, 1):
                r = back(b[k - 1], added(m[k], at + k, r))
            pushed[block * per + q] = r

            def add_sent(slot):
                sent = inbox[pl.ds(pl.multiple_of(first + slot * records, 8), records), :]
                return lambda x: x + reorder(sent, fold[...])

            pushed[block * per + q] = lax.cond(packed & (q == 0), add_sent(1), lambda r: r, r)
            return keep(3, lax.cond(packed & (q == per - 1), add_sent(0), lambda x: x, x))

        return lax.switch(
            table[block, jnp.where(own, quad_own_at, quad_at) + q],
            [functools.partial(plain, block, q), any_seen] + [functools.partial(one_seen, k) for k in range(4)],
            x,
        )

    def filter_oct(block, o, x):
        return lax.cond(
            table[block, jnp.where(block == me, oct_own_at, oct_at) + o] == 0,
            lambda x: plain(block, 2 * o + 1, plain(block, 2 * o, x)),
            lambda x: lax.fori_loop(2 * o, 2 * o + 2, functools.partial(filter_quad, block), x),
            x,
        )

    def filter_block(block, x):
        return lax.fori_loop(0, per // 2, functools.partial(filter_oct, block), x)

    held[0] = first_rows[...]
    x = lax.fori_loop(0, me + 1, filter_block, held[0])
    own_bands = [four(band_at, me, q) for q in range(per)]
    own_masks = [four(mask_at, me, q) for q in range(per)]
    for q in range(per):
        for k in (0, 2):
            at = me * steps + q * 4 + k
            seen = own_masks[q][k] + own_masks[q][k + 1] > 0
            held[at + 1] = jnp.where(seen, held[at + 1], step(own_bands[q][k], held[at]))
    outs = [pltpu.make_async_copy(outward.at[k], smoothed_far.at[:, k], out_sem.at[k]) for k in range(4)]
    outs.append(pltpu.make_async_copy(ready, filtered_far, out_sem.at[4]))
    lax.fori_loop(me + 1, devices, filter_block, x)

    def smooth_quad(block, q, r, gains):
        after[q] = r
        e = gains(block, q, r) + pushed[block * per + q]
        ends[q] = e
        return added(table[block, mask_at + 4 * q], block * steps + 4 * q, e)

    def smooth_all(gains):
        def smooth_block(i, r):
            for q in reversed(range(per)):
                r = smooth_quad(devices - 1 - i, q, r, gains)
            return r

        lax.fori_loop(0, devices - me, smooth_block, jnp.zeros((records, states), F32))

    def smooth_staged():
        high_sum, low_sum = small[0]

        def stage(quad):
            pltpu.matmul_push_rhs(quads[0][quad], 0, 0)
            pltpu.matmul_push_rhs(quads[1][quad], 0, 1)

        def multiply(high, low):
            pltpu.matmul_acc_lhs(high_sum, high, load_staged_rhs=0)
            pltpu.matmul_acc_lhs(low_sum, high, load_staged_rhs=0)
            pltpu.matmul_acc_lhs(high_sum, low)

        def gains(block, q, r):
            multiply(*halves(r))
            stage(jnp.maximum(block * per + q - 1, 0))
            return pltpu.matmul_pop(high_sum) + pltpu.matmul_pop(low_sum)

        stage(devices * per - 1)
        smooth_all(gains)
        none = jnp.zeros((records, states), BF)
        multiply(none, none)
        ends[per] = pltpu.matmul_pop(high_sum) + pltpu.matmul_pop(low_sum)

    if quads:
        smooth_staged()
    else:
        smooth_all(over_quad)

    own_held = held[pl.ds(me * steps + 1, steps)].reshape(steps * records, states)
    ready[...] = reorder(own_held, unfold[...], large).reshape(ready.shape)
    outs[4].start()

    def leave(k, after, staged=False):
        rows_out = jnp.concatenate([held[me * steps + q * 4 + k + 1] + after[q] for q in range(per)], 0)
        outward[k] = reorder(rows_out, unfold[...], staged=staged).reshape(outward.shape[1:])
        outs[k].start()
        return [added(own_masks[q][k], me * steps + q * 4 + k, after[q]) for q in range(per)]

    leave(0, [ends[q] for q in range(per)])
    r = [after[q] for q in range(per)]
    for k in (3, 2, 1):
        b = [own_bands[q][k] for q in range(per)]
        r = leave(k, times_many([(r[q], back_high[b[q]], back_low[b[q]]) for q in range(per)], small, unfold[...]), True)
    for copy in outs:
        copy.wait()


def whole(memory=pltpu.VMEM):
    return pl.BlockSpec(memory_space=memory)


def xor_round(held, low, width, devices):
    return [held] + [
        lax.ppermute(held, "tm", [(i, i ^ (k << low)) for i in range(devices)]) for k in range(1, 1 << width)
    ]


def shards(observations, band_index, obs_mask, diffusivity, gain, back, initial_mean):
    steps, records, states = observations.shape
    bands = diffusivity.shape[0]
    devices = lax.axis_size("tm")
    rows = SLOTS * records + META
    params = pltpu.CompilerParams(vmem_limit_bytes=VMEM_BYTES)
    shape = jax.ShapeDtypeStruct
    message = pl.pallas_call(
        functools.partial(pack_kernel, bands),
        out_shape=shape((rows, states), F32),
        in_specs=[whole(pltpu.HBM)] * 6,
        out_specs=whole(),
        scratch_shapes=[
            pltpu.SMEM((steps,), jnp.int32),
            pltpu.SMEM((steps,), jnp.int32),
            pltpu.VMEM((steps, records, states), F32),
            pltpu.VMEM((bands, states), F32),
            pltpu.VMEM((bands, 8, states), F32),
            pltpu.VMEM((bands, states, states), F32),
            pltpu.VMEM((bands, states, states), F32),
            pltpu.VMEM((steps, records, states), F32),
            pltpu.SemaphoreType.DMA((4,)),
        ],
        compiler_params=pltpu.CompilerParams(vmem_limit_bytes=PACK_VMEM_BYTES),
        name="pack_message",
    )(band_index, obs_mask, observations, diffusivity, gain, back)
    matrix = lambda count: shape((count, states, states), BF)
    cost = lambda flops: pl.CostEstimate(flops=flops, bytes_accessed=4 * 2**20, transcendentals=0)

    def make_tables():
        return pl.pallas_call(
            functools.partial(tables_kernel, bands),
            out_shape=[shape((bands, 8, states), F32), shape((bands * bands, 16, states), F32)]
            + [matrix(bands)] * 6
            + [shape((states, states), BF)] * 2
            + [shape((records, states), F32)],
            in_specs=[whole()] * 4,
            out_specs=[whole()] * 11,
            scratch_shapes=[
                pltpu.VMEM((bands, 5, states // 128, states, 128), F32),
                pltpu.VMEM((bands * 8 + bands * bands * 16 + 8, states), F32),
            ],
            compiler_params=params,
            cost_estimate=cost(2**28),
            name="tables",
        )(diffusivity, gain, back, initial_mean[None, :])

    def make_pairs(back_high, back_low):
        return pl.pallas_call(
            functools.partial(pairs_kernel, bands),
            out_shape=[matrix(bands * bands)] * 2,
            in_specs=[whole()] * 2,
            out_specs=[whole()] * 2,
            compiler_params=params,
            cost_estimate=cost(6 * bands**2 * states**3),
            name="pairs",
        )(back_high, back_low)

    bits = devices.bit_length() - 1
    pieces, fields, low, tables = [message], [], bits, None
    for width in [1] * (bits % 2) + [2] * (bits // 2):
        low -= width
        held = jnp.concatenate(pieces, 0)
        if fields and tables is None:
            tables = make_tables()
            held, tables = lax.optimization_barrier((held, tables))
        pieces = xor_round(held, low, width, devices)
        fields = [(low, 1 << width)] + fields
    tables = make_tables() if tables is None else tables
    tables = [*tables, *make_pairs(*tables[6:8])]
    out = shape((steps // 4, 4, records, states), F32)
    quads = devices * steps // 4
    deep = quads * states * states * 4 <= QUADS_BYTES
    filtered, smoothed = pl.pallas_call(
        functools.partial(main_kernel, bands, devices, fields, len(pieces)),
        out_shape=[out, out],
        in_specs=[whole()] * (1 + len(pieces) + len(tables)),
        out_specs=[whole(pltpu.HBM)] * 2,
        scratch_shapes=[
            pltpu.VMEM((devices * steps + 1, records, states), F32),
            pltpu.VMEM((4, steps // 4, records, states), F32),
            pltpu.VMEM((steps // 4, 4, records, states), F32),
            pltpu.VMEM((steps // 4, records, states), F32),
            pltpu.VMEM((steps // 4 + 1, records, states), F32),
            pltpu.SemaphoreType.DMA((5,)),
            pltpu.VMEM((devices * rows, states), F32),
            pltpu.VMEM((devices, states), jnp.int32),
            pltpu.SMEM((devices, states), jnp.int32),
            pltpu.VMEM((devices * steps, records, states), F32),
            pltpu.VMEM((quads, records, states), F32),
            pltpu.SemaphoreType.DMA,
        ]
        + [pltpu.VMEM((quads, states, states), BF)] * (2 * deep),
        compiler_params=params,
        name="filter_and_smooth",
    )(observations, *pieces, *tables)
    return filtered.reshape(observations.shape), smoothed.reshape(observations.shape)


def solution(mesh):
    return jax.shard_map(
        shards,
        mesh=mesh,
        in_specs=(P("tm", "col", None), P("tm"), P("tm"), P(), P(), P(), P()),
        out_specs=(P("tm", "col", None), P("tm", "col", None)),
        check_vma=False,
    )
```
